768 devices in a mesh: segment: 2 (over core), expert: 48 (over y_hi, z), dp: 8 (over x, y_lo).
Axes of the slice: x: 4, y: 8 (y_hi: 4, y_lo: 2; y = y_hi * 2 + y_lo), z: 12, core: 2. Of those that a mesh axis runs over, the one named last changes fastest.
Arguments:
- moe_input: bfloat16 [2, 6144, 2688], P('segment', 'expert', 'dp'), may hold values from -64 to 64
- norm_gain: float32 [2688], replicated, may hold values from 0.1 to 1.9
- routes: int32 [2, 6144, 6], P('segment', 'expert'), may hold values from 0 to 95, all different within a row; in each aligned block of 128 rows (0 to 127, 128 to 255, ..., all dimensions but the last counted through in order) at most 9 rows name the same one
- route_scores: float32 [2, 6144, 6], P('segment', 'expert'), may hold values from -8 to 8
- w_up: bfloat16 [96, 2688, 1856], P('expert', None, 'dp'), may hold values from -0.125 to 0.125
- w_down: bfloat16 [96, 1856, 2688], P('expert', None, 'dp'), may hold values from -0.125 to 0.125
- queries: bfloat16 [2, 6144, 2048], P('segment', 'expert', 'dp'), may hold values from -100 to 100
- keys: bfloat16 [2, 6144, 256], P('segment', 'expert'), may hold values from -6 to 6
- values: bfloat16 [2, 6144, 256], P('segment', 'expert'), may hold values from -6 to 6
- out_grad: bfloat16 [2, 6144, 2688], P('segment', 'expert'), may hold values from -6 to 6
- w_query: bfloat16 [2688, 2048], P(None, 'dp'), may hold values from -0.125 to 0.125
- w_key: bfloat16 [2688, 256], replicated, may hold values from -0.125 to 0.125
- w_value: bfloat16 [2688, 256], replicated, may hold values from -0.125 to 0.125
- w_out: bfloat16 [2048, 2688], P('dp'), may hold values from -0.125 to 0.125
Outputs:
- moe_next: bfloat16 [2, 6144, 2688], P('segment', 'expert', 'dp')
- grad_prev: bfloat16 [2, 6144, 2688], P('segment', 'expert', 'dp')
The draws below stay inside these ranges and needn't reach their ends.
Inputs may be any that keep to these rules, and one draw needn't show every extreme that they name: `routes`: each row names 6 different experts. Among the 128 rows of one sequence no expert is named more than 9 times, a bound that some block reaches; every expert is named by some row.
All inputs are finite; a program needn't handle non-finite values.
Results may differ from the reference program's by a relative error of at most 0.028.
Values may be sent and summed in bfloat16 or wider, within the bound.
A program may use at most 128 MiB of HBM per device.

```python
import math
import jax
import jax.numpy as jnp
import numpy as np
from jax import lax

D = 2688
HID = 1856
HEADS = 16
KV_HEADS = 2
HEAD_DIM = 128
TOPK = 6
TOK_DEV = 128
SEGMENTS = 2
TOKENS = 6144
EXPERTS = 96
CAP = 9
HEAD_BLOCK = 2
QW = 2048
KVW = 256
N_EXPERT = 48
N_DP = 8


def draw_moe_input(key, part):
    full_shape = (SEGMENTS, TOKENS, D)
    base_key = jax.random.fold_in(key, 21)
    column_key = jax.random.fold_in(key, 22)
    row_key = jax.random.fold_in(key, 23)
    raw_values = jax.random.truncated_normal(base_key, -4.0, 4.0, full_shape, jnp.float32)
    column_scale = jnp.exp(jax.random.uniform(column_key, (SEGMENTS, 1, D), jnp.float32, math.log(0.3), math.log(3.0)))
    row_scale = jnp.exp(jax.random.uniform(row_key, (SEGMENTS, TOKENS, 1), jnp.float32, math.log(0.5), math.log(5.0)))
    return (raw_values * column_scale * row_scale).astype(jnp.bfloat16)


def attention_pair(key):
    sequences = TOKENS // TOK_DEV
    query_key = jax.random.fold_in(key, 31)
    keys_key = jax.random.fold_in(key, 32)
    keys_all = jax.random.truncated_normal(keys_key, -5.0, 5.0, (SEGMENTS, sequences, TOK_DEV, KV_HEADS, HEAD_DIM), jnp.float32)
    queries_all = jax.random.truncated_normal(query_key, -5.0, 5.0, (SEGMENTS, sequences, TOK_DEV, HEADS, HEAD_DIM), jnp.float32)
    return (queries_all.reshape(SEGMENTS, TOKENS, HEADS * HEAD_DIM), keys_all.reshape(SEGMENTS, TOKENS, KV_HEADS * HEAD_DIM))


def draw_queries(key, part):
    return attention_pair(key)[0].astype(jnp.bfloat16)


def draw_keys(key, part):
    return attention_pair(key)[1].astype(jnp.bfloat16)


def level_of(rng, extent, shards, low, top_value):
    def one(dim, blocks):
        heights = jax.random.uniform(jax.random.fold_in(jax.random.fold_in(rng, 6), dim), (blocks,), jnp.float32, low / len(shards), top_value / len(shards))
        return jnp.repeat(jnp.exp(heights), extent[dim] // blocks).reshape((-1,) + (1,) * (len(extent) - dim - 1))

    level = one(*shards[0])
    for cut in shards[1:]:
        level = level * one(*cut)
    return level


def routed_block(rng, own, number, rows, number_of, top, bound, lean):
    order = jax.random.permutation(rng, number_of)
    packed, usual = shares(number_of, rows * top, bound, lean, True), shares(number_of, rows * top, bound, lean, False)
    places = jnp.arange(number_of)

    def named(lengths, offset_by):
        used = int((lengths > 0).sum())
        fixed = max(1, used // 4)
        shifted = fixed + (places - fixed + offset_by * (used - fixed)) % max(1, number_of - fixed)
        return jnp.zeros((number_of,), jnp.int32).at[order[jnp.where(places < fixed, places, shifted)]].set(jnp.asarray(lengths, jnp.int32))

    lengths = jnp.where(number % 4 == 0, named(packed, number // 4), named(usual, number - number // 4 - 1))
    mixed = jax.random.permutation(jax.random.fold_in(own, 3), number_of)
    donor, taker = mixed[0:number_of // 2 * 2:2], mixed[1:number_of // 2 * 2:2]
    margin = jnp.minimum(lengths[donor] - 1, bound - lengths[taker]) // 2
    margin = jnp.where((donor == order[0]) | (taker == order[0]) | (lengths[taker] == 0), 0, jnp.maximum(margin, 0))
    shifted = jax.random.randint(jax.random.fold_in(own, 4), (number_of // 2,), 0, 1 << 20) % (margin + 1)
    lengths = lengths.at[donor].add(-shifted).at[taker].add(shifted)
    members = jnp.searchsorted(jnp.cumsum(lengths), jnp.arange(rows * top), side="right").astype(jnp.int32)
    grid = members.reshape(top, rows).T
    grid = grid[jax.random.permutation(jax.random.fold_in(own, 1), rows)]
    offset_by = jax.random.randint(jax.random.fold_in(own, 2), (rows, 1), 0, top)
    return jnp.take_along_axis(grid, (jnp.arange(top)[None, :] + offset_by) % top, axis=1)


def shares(count, total, reach, slope, full):
    portions = [(1 << 20) // math.isqrt(standing ** slope) + 1 for standing in range(1, count + 1)]
    largest = reach if full else min(reach, max(-(-total // count), total * portions[0] // sum(portions)))
    least = 1 if total - largest >= count - 1 else 0
    counts, rest = [largest] + [least] * (count - 1), total - largest - least * (count - 1)
    while rest > 0:
        movable = [i for i in range(1, count) if counts[i] < largest] or [i for i in range(1, count) if counts[i] < reach]
        whole, remaining = sum([portions[i] for i in movable]), rest
        for i in movable:
            addition = min(reach - counts[i], max(1, remaining * portions[i] // whole), rest)
            counts[i] = counts[i] + addition
            rest = rest - addition
    return np.array(counts)


def noise(own_key, shape, spread, bound, cuts=(), kind=jnp.bfloat16):
    values = spread * jax.random.normal(own_key, shape, jnp.float32)
    if cuts:
        values = values * level_of(own_key, shape, cuts, -0.22, 0.18)
    return jnp.clip(values, -bound, bound).astype(kind)


def setup_inputs(seed: int = 0) -> dict:
    streams_of = jax.random.split(jax.random.key(seed), 15)
    moe_input = draw_moe_input(jax.random.fold_in(streams_of[14], 71), 0)
    norm_gain = jnp.clip(1.0 + 0.18 * jax.random.normal(streams_of[1], (D,), jnp.float32), 0.1, 1.9)
    routes_keys = jax.random.split(jax.random.fold_in(streams_of[2], 1), SEGMENTS * TOKENS // TOK_DEV)
    routes_turns = jax.random.permutation(jax.random.fold_in(streams_of[2], 3), SEGMENTS * TOKENS // TOK_DEV)
    routes = jax.vmap(lambda own, number: routed_block(jax.random.fold_in(streams_of[2], 2), own, number, TOK_DEV, EXPERTS, TOPK, CAP, 2))(routes_keys, routes_turns).reshape((SEGMENTS, TOKENS, TOPK))
    route_scores = noise(streams_of[3], (SEGMENTS, TOKENS, TOPK), 2.0, 8.0, ((0, 2), (1, 48)), jnp.float32)
    w_up = noise(streams_of[4], (EXPERTS, D, HID), D ** -0.5, 0.125, ((0, 48), (2, 8)))
    w_down = noise(streams_of[5], (EXPERTS, HID, D), HID ** -0.5, 0.125, ((0, 48), (2, 8)))
    queries = draw_queries(jax.random.fold_in(streams_of[14], 71), 0)
    keys = draw_keys(jax.random.fold_in(streams_of[14], 71), 0)
    values = noise(streams_of[8], (SEGMENTS, TOKENS, KVW), 1.0, 6.0, ((0, 2), (1, 48)))
    out_grad = noise(streams_of[9], (SEGMENTS, TOKENS, D), 1.0, 6.0, ((0, 2), (1, 48)))
    w_query = noise(streams_of[10], (D, QW), D ** -0.5, 0.125, ((1, 8),))
    w_key = noise(streams_of[11], (D, KVW), D ** -0.5, 0.125)
    w_value = noise(streams_of[12], (D, KVW), D ** -0.5, 0.125)
    w_out = noise(streams_of[13], (QW, D), QW ** -0.5, 0.125, ((0, 8),))
    return {"moe_input": moe_input, "norm_gain": norm_gain, "routes": routes, "route_scores": route_scores, "w_up": w_up, "w_down": w_down, "queries": queries, "keys": keys, "values": values, "out_grad": out_grad, "w_query": w_query, "w_key": w_key, "w_value": w_value, "w_out": w_out}


NORM_EPSILON = 1e-05

def settle(value):
    return lax.optimization_barrier(value.astype(jnp.bfloat16)).astype(jnp.float32)

def slot_places(block_routes):
    flat_routes = block_routes.reshape(-1)
    expert_hits = (flat_routes[:, None] == jnp.arange(EXPERTS, dtype=jnp.int32)[None, :]).astype(jnp.int32)
    earlier = jnp.cumsum(expert_hits, axis=0) - expert_hits
    return lax.optimization_barrier(jnp.sum(earlier * expert_hits, axis=1)).reshape(block_routes.shape).astype(jnp.int32)

def moe_segment(moe_input, norm_gain, routes, route_scores, w_up, w_down):
    input_wide = moe_input.astype(jnp.float32)
    inv_rms = 1.0 / jnp.sqrt(lax.optimization_barrier(jnp.mean(input_wide * input_wide, axis=1)) + NORM_EPSILON)
    scaled = (input_wide * norm_gain[None, :]).astype(jnp.bfloat16)
    signal = jax.nn.sigmoid(route_scores)
    gate_values = settle(signal / lax.optimization_barrier(jnp.sum(signal, axis=1, keepdims=True)))
    blocks = routes.reshape(N_EXPERT, TOK_DEV, TOPK).astype(jnp.int32)
    places = jax.vmap(slot_places)(blocks)
    column = jnp.arange(N_EXPERT, dtype=jnp.int32)[:, None, None]
    token_index = column * TOK_DEV + jnp.arange(TOK_DEV, dtype=jnp.int32)[None, :, None]
    token_index = jnp.broadcast_to(token_index, blocks.shape).astype(jnp.int32)
    slot_index = (column * CAP + places).astype(jnp.int32)
    row_table = jnp.zeros((EXPERTS, N_EXPERT * CAP), jnp.int32).at[blocks, slot_index].set(token_index)
    weight = jnp.zeros((EXPERTS, N_EXPERT * CAP), jnp.float32).at[blocks, slot_index].set(gate_values.reshape(blocks.shape))
    feature_block = D // N_DP

    def per_expert(combined, inputs):
        rows_index, gate_column, up_matrix, down_matrix = inputs
        gathered = scaled[rows_index].astype(jnp.float32)
        pieces = jnp.einsum('rbw,bwh->rbh', gathered.reshape(-1, N_DP, feature_block), up_matrix.reshape(N_DP, feature_block, HID).astype(jnp.float32))
        projected = lax.optimization_barrier(jnp.sum(settle(pieces), axis=1)) * inv_rms[rows_index][:, None]
        hidden = jnp.square(jnp.maximum(projected, 0.0)).astype(jnp.bfloat16)
        expert_out = settle(jnp.dot(hidden, down_matrix, preferred_element_type=jnp.float32))
        return (combined.at[rows_index].add(gate_column[:, None] * expert_out), None)
    combined, _ = lax.scan(per_expert, jnp.zeros((TOKENS, D), jnp.float32), (row_table, weight, w_up, w_down))
    return combined.astype(jnp.bfloat16)

def attention_segment(queries, keys, values, out_grad, w_query, w_key, w_value, w_out):
    sequences = TOKENS // TOK_DEV
    group_size = HEADS // KV_HEADS
    score_scale = HEAD_DIM ** (-0.5)
    d_attn = jnp.dot(out_grad, w_out.T, preferred_element_type=jnp.float32).astype(jnp.bfloat16)
    query_heads = queries.reshape(sequences, TOK_DEV, HEADS, HEAD_DIM).astype(jnp.float32)
    key_heads = jnp.repeat(keys.reshape(sequences, TOK_DEV, KV_HEADS, HEAD_DIM), group_size, axis=2).astype(jnp.float32)
    value_heads = jnp.repeat(values.reshape(sequences, TOK_DEV, KV_HEADS, HEAD_DIM), group_size, axis=2).astype(jnp.float32)
    grad_heads = d_attn.reshape(sequences, TOK_DEV, HEADS, HEAD_DIM).astype(jnp.float32)
    scores = jnp.einsum('sihd,sjhd->shij', query_heads, key_heads) * score_scale
    positions = jnp.arange(TOK_DEV, dtype=jnp.int32)
    causal = positions[None, :] <= positions[:, None]
    scores = jnp.where(causal[None, None], scores, -jnp.inf)
    peak = lax.optimization_barrier(jnp.max(scores, axis=-1, keepdims=True))
    raised = jnp.exp(scores - peak)
    attn_weights = raised / lax.optimization_barrier(jnp.sum(raised, axis=-1, keepdims=True))
    d_weights = jnp.einsum('sihd,sjhd->shij', grad_heads, value_heads)
    row_delta = lax.optimization_barrier(jnp.sum(attn_weights * d_weights, axis=-1, keepdims=True))
    d_scores = settle(attn_weights * (d_weights - row_delta))
    d_query = settle(jnp.einsum('shij,sjhd->sihd', d_scores, key_heads) * score_scale)
    d_key = jnp.einsum('shij,sihd->sjhd', d_scores, query_heads) * score_scale
    d_value = jnp.einsum('shij,sihd->sjhd', settle(attn_weights), grad_heads)
    combined = jnp.zeros((TOKENS, D), jnp.float32)
    for block_index in range(HEADS // HEAD_BLOCK):
        first_head = block_index * HEAD_BLOCK
        head_group = first_head // group_size
        block_query = d_query[:, :, first_head:first_head + HEAD_BLOCK].reshape(TOKENS, HEAD_BLOCK * HEAD_DIM)
        block_key = settle(lax.optimization_barrier(jnp.sum(d_key[:, :, first_head:first_head + HEAD_BLOCK], axis=2))).reshape(TOKENS, HEAD_DIM)
        block_value = settle(lax.optimization_barrier(jnp.sum(d_value[:, :, first_head:first_head + HEAD_BLOCK], axis=2))).reshape(TOKENS, HEAD_DIM)
        query_cols = w_query[:, first_head * HEAD_DIM:(first_head + HEAD_BLOCK) * HEAD_DIM]
        key_cols = w_key[:, head_group * HEAD_DIM:(head_group + 1) * HEAD_DIM]
        value_cols = w_value[:, head_group * HEAD_DIM:(head_group + 1) * HEAD_DIM]
        grad_term = jnp.dot(block_query.astype(jnp.bfloat16), query_cols.T, preferred_element_type=jnp.float32)
        grad_term = grad_term + jnp.dot(block_key.astype(jnp.bfloat16), key_cols.T, preferred_element_type=jnp.float32)
        grad_term = grad_term + jnp.dot(block_value.astype(jnp.bfloat16), value_cols.T, preferred_element_type=jnp.float32)
        combined = combined + settle(grad_term)
    return combined.astype(jnp.bfloat16)

def reference(moe_input, norm_gain, routes, route_scores, w_up, w_down, queries, keys, values, out_grad, w_query, w_key, w_value, w_out):
    moe_parts = [moe_segment(moe_input[segment_index], norm_gain, routes[segment_index], route_scores[segment_index], w_up, w_down) for segment_index in range(SEGMENTS)]
    grad_parts = [attention_segment(queries[segment_index], keys[segment_index], values[segment_index], out_grad[segment_index], w_query, w_key, w_value, w_out) for segment_index in range(SEGMENTS)]
    return (jnp.stack(moe_parts[::-1]), jnp.stack(grad_parts[::-1]))
```

```python
import functools

import jax
import jax.numpy as jnp
from jax import lax
from jax.experimental import pallas as pl
from jax.experimental.pallas import tpu as pltpu
from jax.sharding import Mesh
from jax.sharding import PartitionSpec as P

MESH = pl.DeviceIdType.MESH
F32 = jnp.float32
BF16 = jnp.bfloat16

D = 2688
HID = 1856
HEAD_DIM = 128
TOPK = 6
TOK = 128
CAP = 9
NZ = 12
NYH = 4
NX = 4
FB = 336
FP = 384
HB = 232
HX = 464
HP = 512
SEQS = (7, 5)
ROWS = (64, 48)
FIRST = (0, 7)
LANE_E, LANE_P, LANE_G, LANE_S = 80, 88, 96, 104


def mm(a, b):
    return lax.dot_general(a, b, (((1,), (0,)), ((), ())), preferred_element_type=F32)


def mm_nt(a, b):
    return lax.dot_general(a, b, (((1,), (1,)), ((), ())), preferred_element_type=F32)


def iota(shape, dim):
    return lax.broadcasted_iota(jnp.int32, shape, dim)


def remote(src, dst, sems, index, device):
    return pltpu.make_async_remote_copy(
        src_ref=src,
        dst_ref=dst,
        send_sem=sems[0].at[index],
        recv_sem=sems[1].at[index],
        device_id=device,
        device_id_type=MESH,
    )


def kernel(
    tok_ref, gain_ref, routes_ref, scores_ref, w_up, w_down, queries, keys, values, out_grad,
    w_query, w_key, w_value, w_out,
    moe_out, grad_out,
    ag, sel_a, sel_b, oa, ob, xa, xb, tg, rtg, wu, wuo, wd, wdo, hid_a, hid_b,
    es_a, es_b, ea, eb, mix_a, mix_b, part, rs, gt, gr,
    q_v, k_v, v_v, og_v, wq_v, wkv_v, wo_v, dq_v,
    load_sem,
    ag_s, ag_r, dp_s, dp_r, tg_s, tg_r, w_s, w_r, xg_s, xg_r, hg_s, hg_r, ret_s, ret_r, rs_s, rs_r,
    gr_s, gr_r,
):
    s = lax.axis_index("segment")
    yh = lax.axis_index("yh")
    z = lax.axis_index("z")
    x = lax.axis_index("x")
    yl = lax.axis_index("yl")
    other = 1 - s
    ylo = 1 - yl
    xr, xl = lax.rem(x + 1, NX), lax.rem(x + 3, NX)
    xo = lax.rem(x + 2, NX)
    zr, zl = lax.rem(z + 1, NZ), lax.rem(z + NZ - 1, NZ)
    here = yh * 2 + yl
    sel, o_buf, x_buf, hid = (sel_a, sel_b), (oa, ob), (xa, xb), (hid_a, hid_b)
    es, e_buf, mix = (es_a, es_b), (ea, eb), (mix_a, mix_b)

    barrier = pltpu.get_barrier_semaphore()
    peers = [(s, yh, zr, x, yl), (s, yh, zl, x, yl), (s, yh, z, xr, yl), (s, yh, z, xl, yl)]
    for step in range(4):
        row = lax.rem(yh + step, NYH)
        for o in range(2):
            col = yl if o == 0 else ylo
            peers.append((other, row, z, x, col))
            if step or o:
                peers.append((s, row, z, x, col))
            if step:
                peers.append((other, yh, z, lax.rem(x + step, NX), col))
    for peer in peers:
        pl.semaphore_signal(barrier, inc=1, device_id=peer, device_id_type=MESH)

    group = pl.multiple_of((x // 2) * HEAD_DIM, HEAD_DIM)
    loads = [
        (out_grad, og_v),
        (w_out, wo_v),
        (queries, q_v),
        (keys.at[:, pl.ds(group, HEAD_DIM)], k_v),
        (values.at[:, pl.ds(group, HEAD_DIM)], v_v),
        (w_query, wq_v),
        (w_key.at[:, pl.ds(group, HEAD_DIM)], wkv_v.at[:, pl.ds(0, HEAD_DIM)]),
        (w_value.at[:, pl.ds(group, HEAD_DIM)], wkv_v.at[:, pl.ds(HEAD_DIM, HEAD_DIM)]),
        (w_up.at[yl], wu),
        (w_down.at[yl], wd),
    ]
    loads = [pltpu.make_async_copy(a, b, load_sem.at[i]) for i, (a, b) in enumerate(loads)]
    for load in loads:
        load.start()

    wide = tok_ref[...].astype(F32)
    squares = jnp.sum(wide * wide, axis=1, keepdims=True)
    square_hi = squares.astype(BF16).astype(F32)
    square_lo = squares - square_hi
    scaled = wide * gain_ref[...]
    lanes = iota((TOK, 128), 1)
    rows = iota((TOK, 128), 0)
    chosen = routes_ref[...]
    signal = 1.0 / (1.0 + jnp.exp(-scores_ref[...]))
    gates = signal / jnp.sum(signal, axis=1, keepdims=True)
    hits = jnp.zeros((TOK, 128), F32)
    for k in range(TOPK):
        hits = hits + jnp.where(chosen[:, k : k + 1] == lanes, 1.0, 0.0)
    earlier = mm(jnp.where(lanes < rows, 1.0, 0.0).astype(BF16), hits.astype(BF16)) + 1.0
    tail = scaled[:, 256:]
    for k in range(TOPK):
        expert = chosen[:, k : k + 1]
        place = jnp.sum(jnp.where(expert == lanes, earlier, 0.0), axis=1, keepdims=True)
        tail = jnp.where(lanes == LANE_E + k, expert.astype(F32), tail)
        tail = jnp.where(lanes == LANE_P + k, place, tail)
        tail = jnp.where(lanes == LANE_G + k, gates[:, k : k + 1], tail)
    tail = jnp.where(lanes == LANE_S, square_hi, tail)
    tail = jnp.where(lanes == LANE_S + 1, square_lo, tail)
    ag[0, :, 0:256] = scaled[:, :256].astype(BF16)
    ag[0, :, 256:384] = tail.astype(BF16)
    sel_a[...] = jnp.zeros_like(sel_a)
    sel_b[...] = jnp.zeros_like(sel_b)
    eb[:, 48:64, :] = jnp.zeros((8, 16, FP), BF16)

    pl.semaphore_wait(barrier, len(peers))

    def right(k):
        return remote(ag.at[max(2 * k - 3, 0)], ag.at[2 * k - 1], (ag_s, ag_r), 2 * k - 1, (s, yh, zr, x, yl))

    def left(k):
        return remote(ag.at[2 * k - 2], ag.at[2 * k], (ag_s, ag_r), 2 * k, (s, yh, zl, x, yl))

    sent = []

    def start(copy):
        copy.start()
        sent.append(copy)
        return copy

    hops = {1: (start(right(1)), start(left(1)))}
    half_up, half_down = D // 2, HID // 2
    up_rows = pl.ds(pl.multiple_of(s * half_up, 16), half_up)
    down_rows = pl.ds(pl.multiple_of(s * half_down, 16), half_down)
    swap_up = start(remote(w_up.at[ylo, up_rows], wuo.at[up_rows], (w_s, w_r), 0, (s, yh, z, x, ylo)))

    column = iota((8, 128), 0)
    my_experts = (lax.shift_right_logical(column, 1) * (2 * NZ) + 2 * z + jnp.bitwise_and(column, 1)).astype(F32)

    def take(slot):
        chunk = 0 if slot < FIRST[1] else 1
        at = slot - FIRST[chunk]
        info = jnp.transpose(ag[slot, :, 256:384].astype(F32))
        place = jnp.zeros((8, 128), F32)
        gate = jnp.zeros((8, 128), F32)
        for k in range(TOPK):
            mine = info[LANE_E + k : LANE_E + k + 1, :] == my_experts
            place = place + jnp.where(mine, info[LANE_P + k : LANE_P + k + 1, :], 0.0)
            gate = gate + jnp.where(mine, info[LANE_G + k : LANE_G + k + 1, :], 0.0)
        tg[slot * 16 : slot * 16 + 16, :] = jnp.concatenate([place, gate], axis=0).astype(BF16)
        target = jnp.where(place > 0.0, place + (at * CAP - 1.0), -1.0).astype(jnp.int32)
        count = ROWS[chunk]
        slots = iota((count, 128), 0)
        for y in range(8):
            block = jnp.where(slots == target[y : y + 1, :], 1.0, 0.0).astype(BF16)
            sel[chunk][y * count : (y + 1) * count, at * TOK : (at + 1) * TOK] = block

    def dispatch(chunk):
        n, count = SEQS[chunk], ROWS[chunk]
        blocks = ag[FIRST[chunk] : FIRST[chunk] + n].reshape(n * TOK, FP)
        picked = mm(sel[chunk][...], blocks).astype(BF16)
        o_buf[chunk][...] = picked.reshape(8, count, FP)
        copies = []
        for step in range(4):
            row = lax.rem(yh + step, NYH)
            for o in range(2):
                col = yl if o == 0 else ylo
                copies.append(
                    start(
                        remote(
                            o_buf[chunk].at[row * 2 + col],
                            x_buf[chunk].at[x, yl, pl.ds(pl.multiple_of(yh * count, 16), count)],
                            (dp_s, dp_r),
                            chunk * 8 + step * 2 + o,
                            (other, row, z, x, col),
                        )
                    )
                )
        return copies

    def attention_in():
        for load in loads[:5]:
            load.wait()
        d_attn = mm_nt(og_v[...], wo_v[...]).astype(BF16)
        key, value = k_v[...], v_v[...]
        scale = HEAD_DIM ** (-0.5)
        causal = lanes <= rows
        d_key = jnp.zeros((TOK, HEAD_DIM), F32)
        d_value = jnp.zeros((TOK, HEAD_DIM), F32)
        for h in range(2):
            span = slice(h * HEAD_DIM, (h + 1) * HEAD_DIM)
            query, grad = q_v[:, span], d_attn[:, span]
            score = jnp.where(causal, mm_nt(query, key) * scale, -jnp.inf)
            raised = jnp.exp(score - jnp.max(score, axis=1, keepdims=True))
            weights = raised / jnp.sum(raised, axis=1, keepdims=True)
            d_weights = mm_nt(grad, value)
            delta = jnp.sum(weights * d_weights, axis=1, keepdims=True)
            d_scores = weights * (d_weights - delta)
            dq_v[:, span] = (mm(d_scores.astype(BF16), key) * scale).astype(BF16)
            d_key = d_key + mm(jnp.transpose(d_scores).astype(BF16), query)
            d_value = d_value + mm(jnp.transpose(weights).astype(BF16), grad)
        dq_v[:, 256:384] = (d_key * scale).astype(BF16)
        dq_v[:, 384:512] = d_value.astype(BF16)

    grads = []

    def attention_out(step):
        if step == 0:
            for load in loads[5:8]:
                load.wait()
        to = lax.rem(x + step, NX)
        for o in range(2):
            col = yl if o == 0 else ylo
            block = pl.ds(pl.multiple_of((to * 2 + col) * FB, 16), FB)
            term = mm_nt(dq_v[:, 0:256], wq_v[block, :]) + mm_nt(dq_v[:, 256:512], wkv_v[block, :])
            gt[step * 2 + o, :, 0:FB] = term.astype(BF16)
            grads.append(
                start(remote(gt.at[step * 2 + o], gr.at[step * 2 + o], (gr_s, gr_r), step * 2 + o, (other, yh, z, to, col)))
            )

    def hop(k):
        hops[k][0].wait_recv()
        later = [start(right(k + 1))] if k < 6 else []
        if k < 6:
            hops[k][1].wait_recv()
            if k < 5:
                later.append(start(left(k + 1)))
        hops[k + 1] = tuple(later)

    take(0)
    hop(1)
    take(1)
    take(2)
    attention_in()
    hop(2)
    take(3)
    take(4)
    attention_out(0)
    hop(3)
    take(5)
    take(6)
    arrive_a = dispatch(0)
    hop(4)
    take(7)
    take(8)
    attention_out(1)
    hop(5)
    take(9)
    take(10)
    hop(6)
    take(11)
    arrive_b = dispatch(1)
    table = start(remote(tg, rtg, (tg_s, tg_r), 0, (other, yh, z, x, yl)))
    swap_up.wait_recv()
    share_up = start(remote(wuo.at[up_rows], wuo.at[up_rows], (w_s, w_r), 1, (other, yh, z, x, yl)))
    attention_out(2)
    attention_out(3)

    def spread(buf, sems, chunk):
        a = start(remote(buf.at[x], buf.at[x], sems, chunk * 4, (s, yh, z, xr, yl)))
        b = start(remote(buf.at[x], buf.at[x], sems, chunk * 4 + 1, (s, yh, z, xl, yl)))
        return a, b

    def relay(buf, sems, chunk, nearer, lower, upper):
        nearer[0].wait_recv()
        a = start(remote(buf.at[(xl, *lower)], buf.at[(xl, *lower)], sems, chunk * 4 + 2, (s, yh, z, xr, yl)))
        nearer[1].wait_recv()
        b = start(remote(buf.at[(xr, *upper)], buf.at[(xr, *upper)], sems, chunk * 4 + 3, (s, yh, z, xl, yl)))
        return a, b

    up_sems, hid_sems = (xg_s, xg_r), (hg_s, hg_r)
    for copy in arrive_a:
        copy.wait_recv()
    near_a = spread(xa, up_sems, 0)
    for copy in arrive_b:
        copy.wait_recv()
    near_b = spread(xb, up_sems, 1)
    swap_down = start(remote(w_down.at[ylo, down_rows], wdo.at[down_rows], (w_s, w_r), 2, (s, yh, z, x, ylo)))
    far_a = relay(xa, up_sems, 0, near_a, (0,), (1,))

    table.wait_recv()

    def mixing(slot, turned, base):
        chunk = 0 if slot < FIRST[1] else 1
        at = slot - FIRST[chunk]
        for pair in range(4):
            c = slot * 16 - base + 2 * pair
            low = lanes < 64
            place = jnp.where(low, turned[:, c : c + 1], turned[:, c + 1 : c + 2])
            gate = jnp.where(low, turned[:, c + 8 : c + 9], turned[:, c + 9 : c + 10])
            slots = jnp.bitwise_and(lanes, 63).astype(F32)
            hit = jnp.logical_and(place > 0.0, slots == place + (at * CAP - 1.0))
            mix[chunk][at * TOK : (at + 1) * TOK, pair * 128 : (pair + 1) * 128] = jnp.where(hit, gate, 0.0).astype(BF16)

    turned = jnp.transpose(rtg[0:128, :].astype(F32))
    for slot in range(8):
        mixing(slot, turned, 0)
    turned = jnp.transpose(rtg[64:192, :].astype(F32))
    for slot in range(8, 12):
        mixing(slot, turned, 64)

    loads[8].wait()
    share_up.wait_recv()

    def place_hidden(which):
        return jnp.where(iota((HB, HP), 1) == iota((HB, HP), 0) + which * HB, 1.0, 0.0).astype(BF16)

    def up(chunk, far):
        buf = x_buf[chunk]
        count = 4 * ROWS[chunk]
        mine = jnp.zeros((count, HB), F32)
        theirs = jnp.zeros((count, HB), F32)
        sums = jnp.zeros((count, 128), F32)
        for index, owner in enumerate((x, xl, xr, xo)):
            for part_of in range(2):
                if index == 3:
                    far[part_of].wait_recv()
                first = pl.ds(pl.multiple_of((owner * 2 + part_of) * FB, 16), FB)
                block = buf[owner, part_of, :, 0:FB]
                mine = mine + mm(block, wu[first, :])
                theirs = theirs + mm(block, wuo[first, :])
                sums = sums + buf[owner, part_of, :, 256:384].astype(F32)
        lane = iota((count, 128), 1)
        kept = jnp.where(jnp.logical_or(lane == LANE_S, lane == LANE_S + 1), sums, 0.0)
        inverse = 1.0 / jnp.sqrt(jnp.sum(kept, axis=1, keepdims=True) / D + 1e-5)
        mine = jnp.square(jnp.maximum(mine * inverse, 0.0)).astype(BF16)
        theirs = jnp.square(jnp.maximum(theirs * inverse, 0.0)).astype(BF16)
        hid[chunk][x] = (mm(mine, place_hidden(yl)) + mm(theirs, place_hidden(ylo))).astype(BF16)
        return spread(hid[chunk], hid_sems, chunk)

    hid_near_a = up(0, far_a)
    far_b = relay(xb, up_sems, 1, near_b, (0,), (1,))
    hid_far_a = relay(hid_a, hid_sems, 0, hid_near_a, (pl.ds(0, 128),), (pl.ds(128, 128),))
    hid_near_b = up(1, far_b)
    hid_far_b = relay(hid_b, hid_sems, 1, hid_near_b, (pl.ds(0, 96),), (pl.ds(96, 96),))
    swap_down.wait_recv()
    share_down = start(remote(wdo.at[down_rows], wdo.at[down_rows], (w_s, w_r), 3, (other, yh, z, x, yl)))
    loads[9].wait()
    share_down.wait_recv()

    def down(chunk, far):
        count = ROWS[chunk]
        buf = hid[chunk]
        mine = jnp.zeros((4 * count, FB), F32)
        theirs = jnp.zeros((4 * count, FB), F32)
        for index, owner in enumerate((x, xl, xr, xo)):
            if index == 3:
                far[0].wait_recv()
                far[1].wait_recv()
            first = pl.ds(pl.multiple_of(owner * HX, 16), HX)
            block = buf[owner, :, 0:HX]
            mine = mine + mm(block, wd[first, :])
            theirs = theirs + mm(block, wdo[first, :])
        es[chunk][0, :, 0:FB] = mine.astype(BF16)
        es[chunk][1, :, 0:FB] = theirs.astype(BF16)
        copies = []
        for step in range(4):
            row = lax.rem(yh + step, NYH)
            span = pl.ds(pl.multiple_of(row * count, 16), count)
            for o in range(2):
                source = es[chunk].at[o, span]
                target = e_buf[chunk].at[here, pl.ds(0, count)]
                index = chunk * 8 + step * 2 + o
                if step or o:
                    copies.append(
                        start(remote(source, target, (ret_s, ret_r), index, (s, row, z, x, yl if o == 0 else ylo)))
                    )
                else:
                    local = pltpu.make_async_copy(source, target, ret_r.at[index])
                    local.start()
                    copies.append(local)
        return copies

    def landed(copies):
        copies[0].wait()
        for copy in copies[1:]:
            copy.wait_recv()

    back_a = down(0, hid_far_a)
    back_b = down(1, hid_far_b)

    def combine(chunk):
        n = SEQS[chunk]
        rows_of = e_buf[chunk][...].reshape(512, FP)
        part[FIRST[chunk] : FIRST[chunk] + n] = mm(mix[chunk][...], rows_of).astype(BF16).reshape(n, TOK, FP)

    landed(back_a)
    combine(0)
    landed(back_b)
    combine(1)

    def sum_right(k):
        return remote(part.at[11 if k == 6 else 2 * k], rs.at[k - 1], (rs_s, rs_r), k - 1, (s, yh, zr, x, yl))

    def sum_left(k):
        return remote(part.at[2 * k - 1], rs.at[5 + k], (rs_s, rs_r), 5 + k, (s, yh, zl, x, yl))

    forward = start(sum_right(6))
    backward = start(sum_left(5))
    total = jnp.zeros((TOK, FP), F32)
    for copy in grads[:1]:
        copy.wait_recv()
    total = gr[0].astype(F32)
    for i in range(1, 8):
        grads[i].wait_recv()
        total = total + gr[i].astype(F32)
    grad_out[0] = total[:, :FB].astype(BF16)
    for k in range(5, 0, -1):
        forward.wait_recv()
        part[2 * k] = (part[2 * k].astype(F32) + rs[k].astype(F32)).astype(BF16)
        forward = start(sum_right(k))
        if k > 1:
            backward.wait_recv()
            at = 2 * (k - 1) - 1
            part[at] = (part[at].astype(F32) + rs[5 + k].astype(F32)).astype(BF16)
            backward = start(sum_left(k - 1))
    forward.wait_recv()
    backward.wait_recv()
    total = part[0].astype(F32) + rs[0].astype(F32) + rs[6].astype(F32)
    moe_out[0] = total[:, :FB].astype(BF16)
    for copy in sent:
        copy.wait_send()


def on_device(
    moe_input, norm_gain, routes, route_scores, w_up, w_down, queries, keys, values, out_grad,
    w_query, w_key, w_value, w_out,
):
    tokens = jnp.pad(moe_input[0], ((0, 0), (0, FP - FB)))
    gain = jnp.pad(norm_gain, (0, FP - FB)).reshape(1, FP)
    anywhere = pl.BlockSpec(memory_space=pl.ANY)
    vmem = pl.BlockSpec(memory_space=pltpu.VMEM)
    dma = pltpu.SemaphoreType.DMA

    def vm(*shape):
        return pltpu.VMEM(shape, BF16)

    scratch = [
        vm(12, TOK, FP),
        vm(512, 896), vm(384, 640),
        vm(8, 64, FP), vm(8, 48, FP),
        vm(4, 2, 256, FP), vm(4, 2, 192, FP),
        vm(192, 128), vm(192, 128),
        vm(D, HB), vm(D, HB),
        vm(HID, FB), vm(HID, FB),
        vm(4, 256, HP), vm(4, 192, HP),
        vm(2, 256, FP), vm(2, 192, FP),
        vm(8, 64, FP), vm(8, 64, FP),
        vm(896, 512), vm(640, 512),
        vm(12, TOK, FP), vm(11, TOK, FP),
        vm(8, TOK, FP), vm(8, TOK, FP),
        vm(TOK, 256), vm(TOK, 128), vm(TOK, 128), vm(TOK, D),
        vm(D, 256), vm(D, 256), vm(256, D), vm(TOK, 512),
        dma((10,)),
        dma((12,)), dma((12,)),
        dma((16,)), dma((16,)),
        dma((1,)), dma((1,)),
        dma((4,)), dma((4,)),
        dma((8,)), dma((8,)),
        dma((8,)), dma((8,)),
        dma((16,)), dma((16,)),
        dma((11,)), dma((11,)),
        dma((8,)), dma((8,)),
    ]
    block = jax.ShapeDtypeStruct((1, TOK, FB), BF16)
    return pl.pallas_call(
        kernel,
        name="sections",
        out_shape=(block, block),
        in_specs=[vmem] * 4 + [anywhere] * 10,
        out_specs=(vmem, vmem),
        scratch_shapes=scratch,
        compiler_params=pltpu.CompilerParams(
            collective_id=0, has_side_effects=True, vmem_limit_bytes=56 * 2**20
        ),
    )(
        tokens, gain, routes[0], route_scores[0], w_up, w_down, queries[0], keys[0], values[0], out_grad[0],
        w_query, w_key, w_value, w_out,
    )


def solution(mesh):
    finer = Mesh(
        mesh.devices.reshape(2, NYH, NZ, NX, 2), ("segment", "yh", "z", "x", "yl")
    )
    expert, dp = ("yh", "z"), ("x", "yl")
    return jax.shard_map(
        on_device,
        mesh=finer,
        in_specs=(
            P("segment", expert, dp),
            P(dp),
            P("segment", expert, None),
            P("segment", expert, None),
            P(expert, None, dp),
            P(expert, None, dp),
            P("segment", expert, dp),
            P("segment", expert, None),
            P("segment", expert, None),
            P("segment", expert, None),
            P(None, dp),
            P(),
            P(),
            P(dp, None),
        ),
        out_specs=(P("segment", expert, dp), P("segment", expert, dp)),
        check_vma=False,
    )
```

```python
import jax
import jax.numpy as jnp
from jax import lax
from jax.experimental import pallas as pl
from jax.experimental.pallas import tpu as pltpu
from jax.sharding import Mesh
from jax.sharding import PartitionSpec as P

MESH = pl.DeviceIdType.MESH
F32 = jnp.float32
BF16 = jnp.bfloat16

D = 2688
HID = 1856
HEAD_DIM = 128
TOPK = 6
TOK = 128
CAP = 9
NZ = 12
NYH = 4
NX = 4
FB = 336
FP = 384
HB = 232
HX = 464
HP = 512
SEQS = (7, 5)
ROWS = (64, 48)
FIRST = (0, 7)
LANE_E, LANE_P, LANE_G, LANE_S = 80, 88, 96, 104


def mm(a, b):
    return lax.dot_general(a, b, (((1,), (0,)), ((), ())), preferred_element_type=F32)


def mm_nt(a, b):
    return lax.dot_general(a, b, (((1,), (1,)), ((), ())), preferred_element_type=F32)


def iota(shape, dim):
    return lax.broadcasted_iota(jnp.int32, shape, dim)


def remote(src, dst, sems, index, device):
    return pltpu.make_async_remote_copy(
        src_ref=src,
        dst_ref=dst,
        send_sem=sems[0].at[index],
        recv_sem=sems[1].at[index],
        device_id=device,
        device_id_type=MESH,
    )


def kernel(
    tok_ref, gain_ref, routes_ref, scores_ref, w_up, w_down, queries, keys, values, out_grad,
    w_query, w_key, w_value, w_out,
    moe_out, grad_out,
    ag, sel_a, sel_b, oa, ob, xa, xb, tg, rtg, wut, wuto, wdt, wdto, wu, wuo, wd, wdo, hid_a, hid_b,
    es_a, es_b, ea, eb, mix_a, mix_b, part, rs, gt, gr,
    q_v, k_v, v_v, og_v, wq_v, wkv_v, wo_v, dq_v,
    load_sem,
    ag_s, ag_r, dp_s, dp_r, tg_s, tg_r, w_s, w_r, xg_s, xg_r, hg_s, hg_r, ret_s, ret_r, rs_s, rs_r,
    gr_s, gr_r,
):
    s = lax.axis_index("segment")
    yh = lax.axis_index("yh")
    z = lax.axis_index("z")
    x = lax.axis_index("x")
    yl = lax.axis_index("yl")
    other = 1 - s
    ylo = 1 - yl
    xr, xl = lax.rem(x + 1, NX), lax.rem(x + 3, NX)
    xo = lax.rem(x + 2, NX)
    zr, zl = lax.rem(z + 1, NZ), lax.rem(z + NZ - 1, NZ)
    here = yh * 2 + yl
    sel, o_buf, x_buf, hid = (sel_a, sel_b), (oa, ob), (xa, xb), (hid_a, hid_b)
    es, e_buf, mix = (es_a, es_b), (ea, eb), (mix_a, mix_b)

    barrier = pltpu.get_barrier_semaphore()
    peers = [(s, yh, zr, x, yl), (s, yh, zl, x, yl), (s, yh, z, xr, yl), (s, yh, z, xl, yl)]
    for step in range(4):
        row = lax.rem(yh + step, NYH)
        for o in range(2):
            col = yl if o == 0 else ylo
            peers.append((other, row, z, x, col))
            if step or o:
                peers.append((s, row, z, x, col))
            if step:
                peers.append((other, yh, z, lax.rem(x + step, NX), col))
    for peer in peers:
        pl.semaphore_signal(barrier, inc=1, device_id=peer, device_id_type=MESH)

    group = pl.multiple_of((x // 2) * HEAD_DIM, HEAD_DIM)
    loads = [
        (out_grad, og_v),
        (w_out, wo_v),
        (queries, q_v),
        (keys.at[:, pl.ds(group, HEAD_DIM)], k_v),
        (values.at[:, pl.ds(group, HEAD_DIM)], v_v),
        (w_query, wq_v),
        (w_key.at[:, pl.ds(group, HEAD_DIM)], wkv_v.at[:, pl.ds(0, HEAD_DIM)]),
        (w_value.at[:, pl.ds(group, HEAD_DIM)], wkv_v.at[:, pl.ds(HEAD_DIM, HEAD_DIM)]),
        (w_up.at[yl], wut),
        (w_down.at[yl], wdt),
    ]
    loads = [pltpu.make_async_copy(a, b, load_sem.at[i]) for i, (a, b) in enumerate(loads)]
    for load in loads:
        load.start()

    lanes = iota((TOK, 128), 1)
    rows = iota((TOK, 128), 0)
    wide = tok_ref[...].astype(F32)
    squares = jnp.sum(wide * wide, axis=0, keepdims=True)
    square_hi = squares.astype(BF16).astype(F32)
    square_lo = squares - square_hi
    experts = iota((96, TOK), 0)
    hits = jnp.zeros((96, TOK), F32)
    signals = []
    for k in range(TOPK):
        hits = hits + jnp.where(routes_ref[k] == experts, 1.0, 0.0)
        signals.append(1.0 / (1.0 + jnp.exp(-scores_ref[k])))
    signal_sum = sum(signals[1:], signals[0])
    earlier = mm(hits.astype(BF16), jnp.where(rows < lanes, 1.0, 0.0).astype(BF16)) + 1.0
    info_row = iota((FP - FB, TOK), 0)
    info = jnp.where(info_row == LANE_S - LANE_E, square_hi, 0.0)
    info = jnp.where(info_row == LANE_S - LANE_E + 1, square_lo, info)
    for k in range(TOPK):
        expert = routes_ref[k]
        place = jnp.sum(jnp.where(expert == experts, earlier, 0.0), axis=0, keepdims=True)
        info = jnp.where(info_row == k, expert.astype(F32), info)
        info = jnp.where(info_row == LANE_P - LANE_E + k, place, info)
        info = jnp.where(info_row == LANE_G - LANE_E + k, signals[k] / signal_sum, info)
    gain_at = (x * 2 + yl) * FB
    gain_row, gain_lane = gain_at // 128, lax.rem(gain_at, 128)
    turn = lax.rem(128 - gain_lane, 128)
    pieces = [
        pltpu.roll(jnp.broadcast_to(gain_ref[pl.ds(jnp.minimum(gain_row + i, 20), 1), :], (8, 128)), turn, 1)
        for i in range(4)
    ]
    lane8 = iota((8, 128), 1)
    for i in range(3):
        source = wide[128 * i : 128 * (i + 1)] if i < 2 else jnp.concatenate([wide[256:], info], axis=0)
        gain = jnp.where(lane8 < 128 - gain_lane, pieces[i], pieces[i + 1])
        if i == 2:
            gain = jnp.where(lane8 < LANE_E, gain, 1.0)
        ag[0, :, 128 * i : 128 * (i + 1)] = (jnp.transpose(source) * gain[0:1]).astype(BF16)
    sel_a[...] = jnp.zeros_like(sel_a)
    sel_b[...] = jnp.zeros_like(sel_b)
    eb[:, 48:64, :] = jnp.zeros((8, 16, FP), BF16)

    pl.semaphore_wait(barrier, len(peers))

    def right(k, half):
        span = pl.ds(64 * half, 64)
        source, target = max(2 * k - 3, 0), 2 * k - 1
        return remote(ag.at[source, span], ag.at[target, span], (ag_s, ag_r), 2 * target + half, (s, yh, zr, x, yl))

    def left(k, half):
        span = pl.ds(64 * half, 64)
        source, target = 2 * k - 2, 11 if k == 6 else 2 * k
        return remote(ag.at[source, span], ag.at[target, span], (ag_s, ag_r), 2 * target + half, (s, yh, zl, x, yl))

    sent = []

    def start(copy):
        copy.start()
        sent.append(copy)
        return copy

    def wait_all(*copies):
        for copy in copies:
            copy.wait_recv()

    hops = {}
    for half in range(2):
        hops[1, half] = (start(right(1, half)), start(left(1, half)))
    up_cols = pl.ds(pl.multiple_of(s * 1408, 128), 1280)
    up_middle = pl.ds(1280, 128)
    down_rows = pl.ds(pl.multiple_of(s * 176, 16), 160)
    down_middle = pl.ds(160, 16)
    partner = (s, yh, z, x, ylo)
    swap_up = (
        start(remote(w_up.at[ylo, :, up_cols], wuto.at[:, up_cols], (w_s, w_r), 0, partner)),
        start(remote(w_up.at[ylo, :, up_middle], wuto.at[:, up_middle], (w_s, w_r), 1, partner)),
    )

    column = iota((8, 128), 0)
    my_experts = (lax.shift_right_logical(column, 1) * (2 * NZ) + 2 * z + jnp.bitwise_and(column, 1)).astype(F32)

    def take(slot):
        chunk = 0 if slot < FIRST[1] else 1
        at = slot - FIRST[chunk]
        info = jnp.transpose(ag[slot, :, 256:384].astype(F32))
        place = jnp.zeros((8, 128), F32)
        gate = jnp.zeros((8, 128), F32)
        for k in range(TOPK):
            mine = info[LANE_E + k : LANE_E + k + 1, :] == my_experts
            place = place + jnp.where(mine, info[LANE_P + k : LANE_P + k + 1, :], 0.0)
            gate = gate + jnp.where(mine, info[LANE_G + k : LANE_G + k + 1, :], 0.0)
        tg[slot * 16 : slot * 16 + 16, :] = jnp.concatenate([place, gate], axis=0).astype(BF16)
        target = jnp.where(place > 0.0, place + (at * CAP - 1.0), -1.0).astype(jnp.int32)
        count = ROWS[chunk]
        slots = iota((count, 128), 0)
        for y in range(8):
            block = jnp.where(slots == target[y : y + 1, :], 1.0, 0.0).astype(BF16)
            sel[chunk][y * count : (y + 1) * count, at * TOK : (at + 1) * TOK] = block

    def dispatch(chunk):
        n, count = SEQS[chunk], ROWS[chunk]
        blocks = ag[FIRST[chunk] : FIRST[chunk] + n].reshape(n * TOK, FP)
        picked = mm(sel[chunk][...], blocks).astype(BF16)
        o_buf[chunk][...] = picked.reshape(8, count, FP)
        copies = []
        for step in range(4):
            row = lax.rem(yh + step, NYH)
            for o in range(2):
                col = yl if o == 0 else ylo
                copies.append(
                    start(
                        remote(
                            o_buf[chunk].at[row * 2 + col],
                            x_buf[chunk].at[x, yl, pl.ds(pl.multiple_of(yh * count, 16), count)],
                            (dp_s, dp_r),
                            chunk * 8 + step * 2 + o,
                            (other, row, z, x, col),
                        )
                    )
                )
        return copies

    d_kv = [jnp.zeros((TOK, HEAD_DIM), F32), jnp.zeros((TOK, HEAD_DIM), F32)]
    d_attn = {}

    def attention_grad(h):
        if h == 0:
            for load in loads[:2]:
                load.wait()
        d_attn[h] = mm_nt(og_v[...], wo_v[h * HEAD_DIM : (h + 1) * HEAD_DIM, :]).astype(BF16)

    def attention_in(h):
        if h == 0:
            for load in loads[2:5]:
                load.wait()
        key, value = k_v[...], v_v[...]
        scale = HEAD_DIM ** (-0.5)
        span = slice(h * HEAD_DIM, (h + 1) * HEAD_DIM)
        query, grad = q_v[:, span], d_attn[h]
        score = jnp.where(lanes <= rows, mm_nt(query, key) * scale, -jnp.inf)
        raised = jnp.exp(score - jnp.max(score, axis=1, keepdims=True))
        weights = raised / jnp.sum(raised, axis=1, keepdims=True)
        d_weights = mm_nt(grad, value)
        delta = jnp.sum(weights * d_weights, axis=1, keepdims=True)
        d_scores = weights * (d_weights - delta)
        dq_v[:, span] = (mm(d_scores.astype(BF16), key) * scale).astype(BF16)
        d_kv[0] = d_kv[0] + mm(jnp.transpose(d_scores).astype(BF16), query)
        d_kv[1] = d_kv[1] + mm(jnp.transpose(weights).astype(BF16), grad)
        if h == 1:
            dq_v[:, 256:384] = (d_kv[0] * scale).astype(BF16)
            dq_v[:, 384:512] = d_kv[1].astype(BF16)

    grads = []

    def attention_out(step):
        if step == 0:
            for load in loads[5:8]:
                load.wait()
        to = lax.rem(x + step, NX)
        for o in range(2):
            col = yl if o == 0 else ylo
            block = pl.ds(pl.multiple_of((to * 2 + col) * FB, 16), FB)
            term = mm_nt(dq_v[:, 0:256], wq_v[block, :]) + mm_nt(dq_v[:, 256:512], wkv_v[block, :])
            gt[step * 2 + o, :, 0:FB] = term.astype(BF16)
            grads.append(
                start(remote(gt.at[step * 2 + o], gr.at[step * 2 + o], (gr_s, gr_r), step * 2 + o, (other, yh, z, to, col)))
            )

    def hop(k, half):
        wait_all(*hops[k, half])
        if k < 5:
            hops[k + 1, half] = (start(right(k + 1, half)), start(left(k + 1, half)))
        elif k == 5:
            hops[6, half] = (start(left(6, 1) if half else right(6, 0)),)

    take(0)
    attention_grad(0)
    hop(1, 0)
    hop(1, 1)
    take(1)
    take(2)
    hop(2, 0)
    attention_grad(1)
    hop(2, 1)
    take(3)
    take(4)
    hop(3, 0)
    attention_in(0)
    hop(3, 1)
    take(5)
    take(6)
    arrive_a = dispatch(0)
    hop(4, 0)
    attention_in(1)
    hop(4, 1)
    take(7)
    take(8)
    hop(5, 0)
    attention_out(0)
    hop(5, 1)
    take(9)
    take(10)
    attention_out(1)
    hop(6, 0)
    hop(6, 1)
    take(11)
    arrive_b = dispatch(1)
    table = start(remote(tg, rtg, (tg_s, tg_r), 0, (other, yh, z, x, yl)))
    wait_all(*swap_up)
    share_up = start(remote(wuto.at[:, up_cols], wuto.at[:, up_cols], (w_s, w_r), 2, (other, yh, z, x, yl)))
    attention_out(2)
    attention_out(3)
    unit = jnp.where(lanes == rows, 1.0, 0.0).astype(BF16)

    def turn_up(source, target):
        def step(i, carry):
            span = pl.ds(pl.multiple_of(i * 128, 128), 128)
            target[span, :] = mm_nt(unit, source[:, span]).astype(BF16)
            return carry

        lax.fori_loop(0, D // 128, step, 0)

    def turn_down(source, target):
        def step(i, carry):
            span = pl.ds(pl.multiple_of(i * 128, 128), 128)
            target[span, :] = mm_nt(unit, source[:, span]).astype(BF16)
            return carry

        lax.fori_loop(0, HID // 128, step, 0)
        target[1792:1856, :] = mm_nt(unit[0:64, 0:64], source[:, 1792:1856]).astype(BF16)

    def spread(buf, sems, chunk):
        a = start(remote(buf.at[x], buf.at[x], sems, chunk * 4, (s, yh, z, xr, yl)))
        b = start(remote(buf.at[x], buf.at[x], sems, chunk * 4 + 1, (s, yh, z, xl, yl)))
        return a, b

    def relay(buf, sems, chunk, nearer, lower, upper):
        nearer[0].wait_recv()
        a = start(remote(buf.at[(xl, *lower)], buf.at[(xl, *lower)], sems, chunk * 4 + 2, (s, yh, z, xr, yl)))
        nearer[1].wait_recv()
        b = start(remote(buf.at[(xr, *upper)], buf.at[(xr, *upper)], sems, chunk * 4 + 3, (s, yh, z, xl, yl)))
        return a, b

    up_sems, hid_sems = (xg_s, xg_r), (hg_s, hg_r)
    wait_all(*arrive_a)
    near_a = spread(xa, up_sems, 0)
    loads[8].wait()
    turn_up(wut, wu)
    wait_all(*arrive_b)
    near_b = spread(xb, up_sems, 1)
    swap_down = (
        start(remote(w_down.at[ylo, down_rows], wdto.at[down_rows], (w_s, w_r), 3, partner)),
        start(remote(w_down.at[ylo, down_middle], wdto.at[down_middle], (w_s, w_r), 4, partner)),
    )
    far_a = relay(xa, up_sems, 0, near_a, (0,), (1,))

    table.wait_recv()

    def mixing(slot, turned, base):
        chunk = 0 if slot < FIRST[1] else 1
        at = slot - FIRST[chunk]
        for pair in range(4):
            c = slot * 16 - base + 2 * pair
            low = lanes < 64
            place = jnp.where(low, turned[:, c : c + 1], turned[:, c + 1 : c + 2])
            gate = jnp.where(low, turned[:, c + 8 : c + 9], turned[:, c + 9 : c + 10])
            slots = jnp.bitwise_and(lanes, 63).astype(F32)
            hit = jnp.logical_and(place > 0.0, slots == place + (at * CAP - 1.0))
            mix[chunk][at * TOK : (at + 1) * TOK, pair * 128 : (pair + 1) * 128] = jnp.where(hit, gate, 0.0).astype(BF16)

    turned = jnp.transpose(rtg[0:128, :].astype(F32))
    for slot in range(8):
        mixing(slot, turned, 0)
    turned = jnp.transpose(rtg[64:192, :].astype(F32))
    for slot in range(8, 12):
        mixing(slot, turned, 64)

    share_up.wait_recv()
    turn_up(wuto, wuo)
    far_b = relay(xb, up_sems, 1, near_b, (0,), (1,))

    def place_hidden(which):
        return jnp.where(iota((HB, HP), 1) == iota((HB, HP), 0) + which * HB, 1.0, 0.0).astype(BF16)

    def up(chunk, far):
        buf = x_buf[chunk]
        count = 4 * ROWS[chunk]
        mine = jnp.zeros((count, HB), F32)
        theirs = jnp.zeros((count, HB), F32)
        sums = jnp.zeros((count, 128), F32)
        for index, owner in enumerate((x, xl, xr, xo)):
            for part_of in range(2):
                if index == 3:
                    far[part_of].wait_recv()
                first = pl.ds(pl.multiple_of((owner * 2 + part_of) * FB, 16), FB)
                block = buf[owner, part_of, :, 0:FB]
                mine = mine + mm(block, wu[first, :])
                theirs = theirs + mm(block, wuo[first, :])
                sums = sums + buf[owner, part_of, :, 256:384].astype(F32)
        lane = iota((count, 128), 1)
        kept = jnp.where(jnp.logical_or(lane == LANE_S, lane == LANE_S + 1), sums, 0.0)
        inverse = 1.0 / jnp.sqrt(jnp.sum(kept, axis=1, keepdims=True) / D + 1e-5)
        mine = jnp.square(jnp.maximum(mine * inverse, 0.0)).astype(BF16)
        theirs = jnp.square(jnp.maximum(theirs * inverse, 0.0)).astype(BF16)
        hid[chunk][x] = (mm(mine, place_hidden(yl)) + mm(theirs, place_hidden(ylo))).astype(BF16)
        return spread(hid[chunk], hid_sems, chunk)

    hid_near_a = up(0, far_a)
    hid_near_b = up(1, far_b)
    wait_all(*swap_down)
    share_down = start(remote(wdto.at[down_rows], wdto.at[down_rows], (w_s, w_r), 5, (other, yh, z, x, yl)))
    hid_far_a = relay(hid_a, hid_sems, 0, hid_near_a, (pl.ds(0, 128),), (pl.ds(128, 128),))
    loads[9].wait()
    turn_down(wdt, wd)
    hid_far_b = relay(hid_b, hid_sems, 1, hid_near_b, (pl.ds(0, 96),), (pl.ds(96, 96),))
    share_down.wait_recv()
    turn_down(wdto, wdo)

    def down(chunk, far):
        count = ROWS[chunk]
        buf = hid[chunk]
        mine = jnp.zeros((4 * count, FB), F32)
        theirs = jnp.zeros((4 * count, FB), F32)
        for index, owner in enumerate((x, xl, xr, xo)):
            if index == 3:
                far[0].wait_recv()
                far[1].wait_recv()
            first = pl.ds(pl.multiple_of(owner * HX, 16), HX)
            block = buf[owner, :, 0:HX]
            mine = mine + mm(block, wd[first, :])
            theirs = theirs + mm(block, wdo[first, :])
        es[chunk][0, :, 0:FB] = mine.astype(BF16)
        es[chunk][1, :, 0:FB] = theirs.astype(BF16)
        copies = []
        for step in range(4):
            row = lax.rem(yh + step, NYH)
            span = pl.ds(pl.multiple_of(row * count, 16), count)
            for o in range(2):
                source = es[chunk].at[o, span]
                target = e_buf[chunk].at[here, pl.ds(0, count)]
                index = chunk * 8 + step * 2 + o
                if step or o:
                    copies.append(
                        start(remote(source, target, (ret_s, ret_r), index, (s, row, z, x, yl if o == 0 else ylo)))
                    )
                else:
                    local = pltpu.make_async_copy(source, target, ret_r.at[index])
                    local.start()
                    copies.append(local)
        return copies

    def landed(copies):
        copies[0].wait()
        for copy in copies[1:]:
            copy.wait_recv()

    back_a = down(0, hid_far_a)
    back_b = down(1, hid_far_b)

    def combine(chunk):
        n = SEQS[chunk]
        rows_of = e_buf[chunk][...].reshape(512, FP)
        part[FIRST[chunk] : FIRST[chunk] + n] = mm(mix[chunk][...], rows_of).astype(BF16).reshape(n, TOK, FP)

    landed(back_a)
    combine(0)
    landed(back_b)
    combine(1)

    def sum_right(k, half):
        span = pl.ds(64 * half, 64)
        source = part.at[11 if k == 6 else 2 * k, span]
        return remote(source, rs.at[k - 1, span], (rs_s, rs_r), 2 * (k - 1) + half, (s, yh, zr, x, yl))

    def sum_left(k, half):
        span = pl.ds(64 * half, 64)
        source = part.at[11 if k == 6 else 2 * k - 1, span]
        return remote(source, rs.at[5 + k, span], (rs_s, rs_r), 2 * (5 + k) + half, (s, yh, zl, x, yl))

    def add(slot, arrived, half):
        span = slice(64 * half, 64 * half + 64)
        part[slot, span] = (part[slot, span].astype(F32) + rs[arrived, span].astype(F32)).astype(BF16)

    forward = {0: start(sum_right(6, 0)), 1: start(sum_right(5, 1))}
    backward = {1: start(sum_left(6, 1)), 0: start(sum_left(5, 0))}

    def write(out, total):
        for i in range(3):
            column_block = jnp.transpose(total[:, 128 * i : 128 * (i + 1)]).astype(BF16)
            out[128 * i : min(128 * (i + 1), FB), :] = column_block if i < 2 else column_block[0 : FB - 256]

    wait_all(*grads)
    total = gr[0].astype(F32)
    for i in range(1, 8):
        total = total + gr[i].astype(F32)
    write(grad_out, total)
    for k in range(5, 0, -1):
        for half in range(2):
            if k < 5 or half == 0:
                forward[half].wait_recv()
                add(2 * k, k, half)
                forward[half] = start(sum_right(k, half))
            if k < 5 or half == 1:
                backward[half].wait_recv()
                add(2 * k - 1, 6 + k, half)
                backward[half] = start(sum_left(k, half))
    wait_all(forward[0], backward[0], forward[1], backward[1])
    write(moe_out, part[0].astype(F32) + rs[0].astype(F32) + rs[6].astype(F32))
    for copy in sent:
        copy.wait_send()


def on_device(
    moe_input, norm_gain, routes, route_scores, w_up, w_down, queries, keys, values, out_grad,
    w_query, w_key, w_value, w_out,
):
    tokens = jnp.transpose(moe_input[0])
    gain = norm_gain.reshape(D // 128, 128)
    routes, route_scores = jnp.transpose(routes, (2, 0, 1)), jnp.transpose(route_scores, (2, 0, 1))
    w_up, w_down = jnp.transpose(w_up, (0, 2, 1)), jnp.transpose(w_down, (0, 2, 1))
    anywhere = pl.BlockSpec(memory_space=pl.ANY)
    vmem = pl.BlockSpec(memory_space=pltpu.VMEM)
    dma = pltpu.SemaphoreType.DMA

    def vm(*shape):
        return pltpu.VMEM(shape, BF16)

    scratch = [
        vm(12, TOK, FP),
        vm(512, 896), vm(384, 640),
        vm(8, 64, FP), vm(8, 48, FP),
        vm(4, 2, 256, FP), vm(4, 2, 192, FP),
        vm(192, 128), vm(192, 128),
        vm(HB, D), vm(HB, D), vm(FB, HID), vm(FB, HID),
        vm(D, HB), vm(D, HB),
        vm(HID, FB), vm(HID, FB),
        vm(4, 256, HP), vm(4, 192, HP),
        vm(2, 256, FP), vm(2, 192, FP),
        vm(8, 64, FP), vm(8, 64, FP),
        vm(896, 512), vm(640, 512),
        vm(12, TOK, FP), vm(12, TOK, FP),
        vm(8, TOK, FP), vm(8, TOK, FP),
        vm(TOK, 256), vm(TOK, 128), vm(TOK, 128), vm(TOK, D),
        vm(D, 256), vm(D, 256), vm(256, D), vm(TOK, 512),
        dma((10,)),
        dma((24,)), dma((24,)),
        dma((16,)), dma((16,)),
        dma((1,)), dma((1,)),
        dma((6,)), dma((6,)),
        dma((8,)), dma((8,)),
        dma((8,)), dma((8,)),
        dma((16,)), dma((16,)),
        dma((24,)), dma((24,)),
        dma((8,)), dma((8,)),
    ]
    block = jax.ShapeDtypeStruct((FB, TOK), BF16)
    moe_next, grad_prev = pl.pallas_call(
        kernel,
        name="sections",
        out_shape=(block, block),
        in_specs=[vmem] * 4 + [anywhere] * 10,
        out_specs=(vmem, vmem),
        scratch_shapes=scratch,
        compiler_params=pltpu.CompilerParams(
            collective_id=0, has_side_effects=True, vmem_limit_bytes=56 * 2**20
        ),
    )(
        tokens, gain, routes, route_scores, w_up, w_down, queries[0], keys[0], values[0], out_grad[0],
        w_query, w_key, w_value, w_out,
    )
    return jnp.transpose(moe_next)[None], jnp.transpose(grad_prev)[None]


def solution(mesh):
    finer = Mesh(
        mesh.devices.reshape(2, NYH, NZ, NX, 2), ("segment", "yh", "z", "x", "yl")
    )
    expert, dp = ("yh", "z"), ("x", "yl")
    return jax.shard_map(
        on_device,
        mesh=finer,
        in_specs=(
            P("segment", expert, dp),
            P(),
            P("segment", expert, None),
            P("segment", expert, None),
            P(expert, None, dp),
            P(expert, None, dp),
            P("segment", expert, dp),
            P("segment", expert, None),
            P("segment", expert, None),
            P("segment", expert, None),
            P(None, dp),
            P(),
            P(),
            P(dp, None),
        ),
        out_specs=(P("segment", expert, dp), P("segment", expert, dp)),
        check_vma=False,
    )
```

```python
import jax
import jax.numpy as jnp
from jax import lax
from jax.experimental import pallas as pl
from jax.experimental.pallas import tpu as pltpu
from jax.sharding import Mesh
from jax.sharding import PartitionSpec as P

MESH = pl.DeviceIdType.MESH
F32 = jnp.float32
BF16 = jnp.bfloat16

D = 2688
HID = 1856
HEAD_DIM = 128
TOPK = 6
TOK = 128
CAP = 9
NZ = 12
NYH = 4
NX = 4
FB = 336
FP = 384
HB = 232
HX = 464
HP = 512
SEQS = (7, 5)
ROWS = (64, 48)
FIRST = (0, 7)
LANE_E, LANE_P, LANE_G, LANE_S = 80, 88, 96, 104


def mm(a, b):
    return lax.dot_general(a, b, (((1,), (0,)), ((), ())), preferred_element_type=F32)


def mm_nt(a, b):
    return lax.dot_general(a, b, (((1,), (1,)), ((), ())), preferred_element_type=F32)


def iota(shape, dim):
    return lax.broadcasted_iota(jnp.int32, shape, dim)


def remote(src, dst, sems, index, device):
    return pltpu.make_async_remote_copy(
        src_ref=src,
        dst_ref=dst,
        send_sem=sems[0].at[index],
        recv_sem=sems[1].at[index],
        device_id=device,
        device_id_type=MESH,
    )


def kernel(
    tok_ref, gain_ref, routes_ref, scores_ref, w_up, w_down, queries, keys, values, out_grad,
    w_query, w_key, w_value, w_out,
    moe_out, grad_out,
    ag, sel_a, sel_b, oa, ob, xa, xb, tg, rtg, wut, wuto, wdt, wdto, wu, wuo, wd, wdo, hid_a, hid_b,
    es_a, es_b, ea, eb, mix_a, mix_b, part, rs, gt, gr,
    q_v, k_v, v_v, og_v, wq_v, wkv_v, wo_v, dq_v,
    load_sem,
    ag_s, ag_r, dp_s, dp_r, tg_s, tg_r, w_s, w_r, xg_s, xg_r, hg_s, hg_r, ret_s, ret_r, rs_s, rs_r,
    gr_s, gr_r,
):
    s = lax.axis_index("segment")
    yh = lax.axis_index("yh")
    z = lax.axis_index("z")
    x = lax.axis_index("x")
    yl = lax.axis_index("yl")
    other = 1 - s
    ylo = 1 - yl
    xr, xl = lax.rem(x + 1, NX), lax.rem(x + 3, NX)
    xo = lax.rem(x + 2, NX)
    zr, zl = lax.rem(z + 1, NZ), lax.rem(z + NZ - 1, NZ)
    here = yh * 2 + yl
    sel, o_buf, x_buf, hid = (sel_a, sel_b), (oa, ob), (xa, xb), (hid_a, hid_b)
    es, e_buf, mix = (es_a, es_b), (ea, eb), (mix_a, mix_b)

    barrier = pltpu.get_barrier_semaphore()
    peers = [(s, yh, zr, x, yl), (s, yh, zl, x, yl), (s, yh, z, xr, yl), (s, yh, z, xl, yl)]
    for step in range(4):
        row = lax.rem(yh + step, NYH)
        for o in range(2):
            col = yl if o == 0 else ylo
            peers.append((other, row, z, x, col))
            if step or o:
                peers.append((s, row, z, x, col))
            if step:
                peers.append((other, yh, z, lax.rem(x + step, NX), col))
    for peer in peers:
        pl.semaphore_signal(barrier, inc=1, device_id=peer, device_id_type=MESH)

    group = pl.multiple_of((x // 2) * HEAD_DIM, HEAD_DIM)
    loads = [
        (out_grad, og_v),
        (w_out, wo_v),
        (queries, q_v),
        (keys.at[:, pl.ds(group, HEAD_DIM)], k_v),
        (values.at[:, pl.ds(group, HEAD_DIM)], v_v),
        (w_query, wq_v),
        (w_key.at[:, pl.ds(group, HEAD_DIM)], wkv_v.at[:, pl.ds(0, HEAD_DIM)]),
        (w_value.at[:, pl.ds(group, HEAD_DIM)], wkv_v.at[:, pl.ds(HEAD_DIM, HEAD_DIM)]),
        (w_up.at[yl], wut),
        (w_down.at[yl], wdt),
    ]
    loads = [pltpu.make_async_copy(a, b, load_sem.at[i]) for i, (a, b) in enumerate(loads)]
    for load in loads:
        load.start()

    lanes = iota((TOK, 128), 1)
    rows = iota((TOK, 128), 0)
    wide = tok_ref[...].astype(F32)
    squares = jnp.sum(wide * wide, axis=0, keepdims=True)
    square_hi = squares.astype(BF16).astype(F32)
    square_lo = squares - square_hi
    experts = iota((96, TOK), 0)
    hits = jnp.zeros((96, TOK), F32)
    signals = []
    for k in range(TOPK):
        hits = hits + jnp.where(routes_ref[k] == experts, 1.0, 0.0)
        signals.append(1.0 / (1.0 + jnp.exp(-scores_ref[k])))
    signal_sum = sum(signals[1:], signals[0])
    earlier = mm(hits.astype(BF16), jnp.where(rows < lanes, 1.0, 0.0).astype(BF16)) + 1.0
    info_row = iota((FP - FB, TOK), 0)
    info = jnp.where(info_row == LANE_S - LANE_E, square_hi, 0.0)
    info = jnp.where(info_row == LANE_S - LANE_E + 1, square_lo, info)
    for k in range(TOPK):
        expert = routes_ref[k]
        place = jnp.sum(jnp.where(expert == experts, earlier, 0.0), axis=0, keepdims=True)
        info = jnp.where(info_row == k, expert.astype(F32), info)
        info = jnp.where(info_row == LANE_P - LANE_E + k, place, info)
        info = jnp.where(info_row == LANE_G - LANE_E + k, signals[k] / signal_sum, info)
    gain_at = (x * 2 + yl) * FB
    gain_row, gain_lane = gain_at // 128, lax.rem(gain_at, 128)
    turn = lax.rem(128 - gain_lane, 128)
    pieces = [
        pltpu.roll(jnp.broadcast_to(gain_ref[pl.ds(jnp.minimum(gain_row + i, 20), 1), :], (8, 128)), turn, 1)
        for i in range(4)
    ]
    lane8 = iota((8, 128), 1)
    for i in range(3):
        source = wide[128 * i : 128 * (i + 1)] if i < 2 else jnp.concatenate([wide[256:], info], axis=0)
        gain = jnp.where(lane8 < 128 - gain_lane, pieces[i], pieces[i + 1])
        if i == 2:
            gain = jnp.where(lane8 < LANE_E, gain, 1.0)
        ag[0, :, 128 * i : 128 * (i + 1)] = (jnp.transpose(source) * gain[0:1]).astype(BF16)
    sel_a[...] = jnp.zeros_like(sel_a)
    sel_b[...] = jnp.zeros_like(sel_b)
    eb[:, 48:64, :] = jnp.zeros((8, 16, FP), BF16)

    pl.semaphore_wait(barrier, len(peers))

    def right(k, half):
        span = pl.ds(64 * half, 64)
        source, target = max(2 * k - 3, 0), 2 * k - 1
        return remote(ag.at[source, span], ag.at[target, span], (ag_s, ag_r), 2 * target + half, (s, yh, zr, x, yl))

    def left(k, half):
        span = pl.ds(64 * half, 64)
        source, target = 2 * k - 2, 11 if k == 6 else 2 * k
        return remote(ag.at[source, span], ag.at[target, span], (ag_s, ag_r), 2 * target + half, (s, yh, zl, x, yl))

    sent = []

    def start(copy):
        copy.start()
        sent.append(copy)
        return copy

    def wait_all(*copies):
        for copy in copies:
            copy.wait_recv()

    hops = {}
    for half in range(2):
        hops[1, half] = (start(right(1, half)), start(left(1, half)))
    up_cols = pl.ds(pl.multiple_of(s * 1408, 128), 1280)
    up_middle = pl.ds(1280, 128)
    down_rows = pl.ds(pl.multiple_of(s * 176, 16), 160)
    down_middle = pl.ds(160, 16)
    partner = (s, yh, z, x, ylo)
    swap_up = (
        start(remote(w_up.at[ylo, :, up_cols], wuto.at[:, up_cols], (w_s, w_r), 0, partner)),
        start(remote(w_up.at[ylo, :, up_middle], wuto.at[:, up_middle], (w_s, w_r), 1, partner)),
    )

    column = iota((8, 128), 0)
    my_experts = (lax.shift_right_logical(column, 1) * (2 * NZ) + 2 * z + jnp.bitwise_and(column, 1)).astype(F32)

    def take(slot):
        chunk = 0 if slot < FIRST[1] else 1
        at = slot - FIRST[chunk]
        info = jnp.transpose(ag[slot, :, 256:384].astype(F32))
        place = jnp.zeros((8, 128), F32)
        gate = jnp.zeros((8, 128), F32)
        for k in range(TOPK):
            mine = info[LANE_E + k : LANE_E + k + 1, :] == my_experts
            place = place + jnp.where(mine, info[LANE_P + k : LANE_P + k + 1, :], 0.0)
            gate = gate + jnp.where(mine, info[LANE_G + k : LANE_G + k + 1, :], 0.0)
        tg[slot * 16 : slot * 16 + 16, :] = jnp.concatenate([place, gate], axis=0).astype(BF16)
        target = jnp.where(place > 0.0, place + (at * CAP - 1.0), -1.0).astype(jnp.int32)
        count = ROWS[chunk]
        slots = iota((count, 128), 0)
        for y in range(8):
            block = jnp.where(slots == target[y : y + 1, :], 1.0, 0.0).astype(BF16)
            sel[chunk][y * count : (y + 1) * count, at * TOK : (at + 1) * TOK] = block

    def dispatch(chunk):
        n, count = SEQS[chunk], ROWS[chunk]
        blocks = ag[FIRST[chunk] : FIRST[chunk] + n].reshape(n * TOK, FP)
        picked = mm(sel[chunk][...], blocks).astype(BF16)
        o_buf[chunk][...] = picked.reshape(8, count, FP)
        copies = []
        for step in range(4):
            row = lax.rem(yh + step, NYH)
            for o in range(2):
                col = yl if o == 0 else ylo
                copies.append(
                    start(
                        remote(
                            o_buf[chunk].at[row * 2 + col],
                            x_buf[chunk].at[x, yl, pl.ds(pl.multiple_of(yh * count, 16), count)],
                            (dp_s, dp_r),
                            chunk * 8 + step * 2 + o,
                            (other, row, z, x, col),
                        )
                    )
                )
        return copies

    d_kv = [jnp.zeros((TOK, HEAD_DIM), F32), jnp.zeros((TOK, HEAD_DIM), F32)]
    d_attn = {}

    def attention_grad(h):
        if h == 0:
            for load in loads[:2]:
                load.wait()
        d_attn[h] = mm_nt(og_v[...], wo_v[h * HEAD_DIM : (h + 1) * HEAD_DIM, :]).astype(BF16)

    def attention_in(h):
        if h == 0:
            for load in loads[2:5]:
                load.wait()
        key, value = k_v[...], v_v[...]
        scale = HEAD_DIM ** (-0.5)
        span = slice(h * HEAD_DIM, (h + 1) * HEAD_DIM)
        query, grad = q_v[:, span], d_attn[h]
        score = jnp.where(lanes <= rows, mm_nt(query, key) * scale, -jnp.inf)
        raised = jnp.exp(score - jnp.max(score, axis=1, keepdims=True))
        weights = raised / jnp.sum(raised, axis=1, keepdims=True)
        d_weights = mm_nt(grad, value)
        delta = jnp.sum(weights * d_weights, axis=1, keepdims=True)
        d_scores = weights * (d_weights - delta)
        dq_v[:, span] = (mm(d_scores.astype(BF16), key) * scale).astype(BF16)
        d_kv[0] = d_kv[0] + mm(jnp.transpose(d_scores).astype(BF16), query)
        d_kv[1] = d_kv[1] + mm(jnp.transpose(weights).astype(BF16), grad)
        if h == 1:
            dq_v[:, 256:384] = (d_kv[0] * scale).astype(BF16)
            dq_v[:, 384:512] = d_kv[1].astype(BF16)

    grads = []

    def attention_out(step):
        if step == 2:
            for load in loads[5:8]:
                load.wait()
        to = lax.rem(x + step, NX)
        for o in range(2):
            col = yl if o == 0 else ylo
            block = pl.ds(pl.multiple_of((to * 2 + col) * FB, 16), FB)
            term = mm_nt(dq_v[:, 0:256], wq_v[block, :]) + mm_nt(dq_v[:, 256:512], wkv_v[block, :])
            gt[step * 2 + o, :, 0:FB] = term.astype(BF16)
            grads.append(
                start(remote(gt.at[step * 2 + o], gr.at[step * 2 + o], (gr_s, gr_r), step * 2 + o, (other, yh, z, to, col)))
            )

    def hop(k, half):
        wait_all(*hops[k, half])
        if k < 5:
            hops[k + 1, half] = (start(right(k + 1, half)), start(left(k + 1, half)))
        elif k == 5:
            hops[6, half] = (start(left(6, 1) if half else right(6, 0)),)

    take(0)
    attention_grad(0)
    hop(1, 0)
    hop(1, 1)
    take(1)
    take(2)
    hop(2, 0)
    attention_grad(1)
    hop(2, 1)
    take(3)
    take(4)
    hop(3, 0)
    attention_in(0)
    hop(3, 1)
    take(5)
    take(6)
    arrive_a = dispatch(0)
    hop(4, 0)
    attention_in(1)
    hop(4, 1)
    take(7)
    take(8)
    hop(5, 0)
    attention_out(2)
    hop(5, 1)
    take(9)
    take(10)
    attention_out(1)
    hop(6, 0)
    hop(6, 1)
    take(11)
    arrive_b = dispatch(1)
    table = start(remote(tg, rtg, (tg_s, tg_r), 0, (other, yh, z, x, yl)))
    wait_all(*swap_up)
    share_up = start(remote(wuto.at[:, up_cols], wuto.at[:, up_cols], (w_s, w_r), 2, (other, yh, z, x, yl)))
    attention_out(3)
    attention_out(0)
    unit = jnp.where(lanes == rows, 1.0, 0.0).astype(BF16)

    def turn_up(source, target):
        def step(i, carry):
            span = pl.ds(pl.multiple_of(i * 128, 128), 128)
            target[span, :] = mm_nt(unit, source[:, span]).astype(BF16)
            return carry

        lax.fori_loop(0, D // 128, step, 0)

    def turn_down(source, target):
        def step(i, carry):
            span = pl.ds(pl.multiple_of(i * 128, 128), 128)
            target[span, :] = mm_nt(unit, source[:, span]).astype(BF16)
            return carry

        lax.fori_loop(0, HID // 128, step, 0)
        target[1792:1856, :] = mm_nt(unit[0:64, 0:64], source[:, 1792:1856]).astype(BF16)

    def spread(buf, sems, chunk):
        a = start(remote(buf.at[x], buf.at[x], sems, chunk * 4, (s, yh, z, xr, yl)))
        b = start(remote(buf.at[x], buf.at[x], sems, chunk * 4 + 1, (s, yh, z, xl, yl)))
        return a, b

    def relay(buf, sems, chunk, nearer, lower, upper):
        nearer[0].wait_recv()
        a = start(remote(buf.at[(xl, *lower)], buf.at[(xl, *lower)], sems, chunk * 4 + 2, (s, yh, z, xr, yl)))
        nearer[1].wait_recv()
        b = start(remote(buf.at[(xr, *upper)], buf.at[(xr, *upper)], sems, chunk * 4 + 3, (s, yh, z, xl, yl)))
        return a, b

    up_sems, hid_sems = (xg_s, xg_r), (hg_s, hg_r)
    wait_all(*arrive_a)
    near_a = spread(xa, up_sems, 0)
    loads[8].wait()
    turn_up(wut, wu)
    wait_all(*arrive_b)
    near_b = spread(xb, up_sems, 1)
    swap_down = (
        start(remote(w_down.at[ylo, down_rows], wdto.at[down_rows], (w_s, w_r), 3, partner)),
        start(remote(w_down.at[ylo, down_middle], wdto.at[down_middle], (w_s, w_r), 4, partner)),
    )
    far_a = relay(xa, up_sems, 0, near_a, (0,), (1,))

    table.wait_recv()

    def mixing(slot, turned, base):
        chunk = 0 if slot < FIRST[1] else 1
        at = slot - FIRST[chunk]
        for pair in range(4):
            c = slot * 16 - base + 2 * pair
            low = lanes < 64
            place = jnp.where(low, turned[:, c : c + 1], turned[:, c + 1 : c + 2])
            gate = jnp.where(low, turned[:, c + 8 : c + 9], turned[:, c + 9 : c + 10])
            slots = jnp.bitwise_and(lanes, 63).astype(F32)
            hit = jnp.logical_and(place > 0.0, slots == place + (at * CAP - 1.0))
            mix[chunk][at * TOK : (at + 1) * TOK, pair * 128 : (pair + 1) * 128] = jnp.where(hit, gate, 0.0).astype(BF16)

    turned = jnp.transpose(rtg[0:128, :].astype(F32))
    for slot in range(8):
        mixing(slot, turned, 0)
    turned = jnp.transpose(rtg[64:192, :].astype(F32))
    for slot in range(8, 12):
        mixing(slot, turned, 64)

    share_up.wait_recv()
    turn_up(wuto, wuo)
    far_b = relay(xb, up_sems, 1, near_b, (0,), (1,))

    def place_hidden(which):
        return jnp.where(iota((HB, HP), 1) == iota((HB, HP), 0) + which * HB, 1.0, 0.0).astype(BF16)

    def up(chunk, far):
        buf = x_buf[chunk]
        count = 4 * ROWS[chunk]
        mine = jnp.zeros((count, HB), F32)
        theirs = jnp.zeros((count, HB), F32)
        sums = jnp.zeros((count, 128), F32)
        for index, owner in enumerate((x, xl, xr, xo)):
            for part_of in range(2):
                if index == 3:
                    far[part_of].wait_recv()
                first = pl.ds(pl.multiple_of((owner * 2 + part_of) * FB, 16), FB)
                block = buf[owner, part_of, :, 0:FB]
                mine = mine + mm(block, wu[first, :])
                theirs = theirs + mm(block, wuo[first, :])
                sums = sums + buf[owner, part_of, :, 256:384].astype(F32)
        lane = iota((count, 128), 1)
        kept = jnp.where(jnp.logical_or(lane == LANE_S, lane == LANE_S + 1), sums, 0.0)
        inverse = 1.0 / jnp.sqrt(jnp.sum(kept, axis=1, keepdims=True) / D + 1e-5)
        mine = jnp.square(jnp.maximum(mine * inverse, 0.0)).astype(BF16)
        theirs = jnp.square(jnp.maximum(theirs * inverse, 0.0)).astype(BF16)
        hid[chunk][x] = (mm(mine, place_hidden(yl)) + mm(theirs, place_hidden(ylo))).astype(BF16)
        return spread(hid[chunk], hid_sems, chunk)

    hid_near_a = up(0, far_a)
    hid_near_b = up(1, far_b)
    wait_all(*swap_down)
    share_down = start(remote(wdto.at[down_rows], wdto.at[down_rows], (w_s, w_r), 5, (other, yh, z, x, yl)))
    hid_far_a = relay(hid_a, hid_sems, 0, hid_near_a, (pl.ds(0, 128),), (pl.ds(128, 128),))
    loads[9].wait()
    turn_down(wdt, wd)
    hid_far_b = relay(hid_b, hid_sems, 1, hid_near_b, (pl.ds(0, 96),), (pl.ds(96, 96),))
    share_down.wait_recv()
    turn_down(wdto, wdo)

    def down(chunk, far):
        count = ROWS[chunk]
        buf = hid[chunk]
        mine = jnp.zeros((4 * count, FB), F32)
        theirs = jnp.zeros((4 * count, FB), F32)
        for index, owner in enumerate((x, xl, xr, xo)):
            if index == 3:
                far[0].wait_recv()
                far[1].wait_recv()
            first = pl.ds(pl.multiple_of(owner * HX, 16), HX)
            block = buf[owner, :, 0:HX]
            mine = mine + mm(block, wd[first, :])
            theirs = theirs + mm(block, wdo[first, :])
        es[chunk][0, :, 0:FB] = mine.astype(BF16)
        es[chunk][1, :, 0:FB] = theirs.astype(BF16)
        copies = []
        for step in range(4):
            row = lax.rem(yh + step, NYH)
            span = pl.ds(pl.multiple_of(row * count, 16), count)
            for o in range(2):
                source = es[chunk].at[o, span]
                target = e_buf[chunk].at[here, pl.ds(0, count)]
                index = chunk * 8 + step * 2 + o
                if step or o:
                    copies.append(
                        start(remote(source, target, (ret_s, ret_r), index, (s, row, z, x, yl if o == 0 else ylo)))
                    )
                else:
                    local = pltpu.make_async_copy(source, target, ret_r.at[index])
                    local.start()
                    copies.append(local)
        return copies

    def landed(copies):
        copies[0].wait()
        for copy in copies[1:]:
            copy.wait_recv()

    back_a = down(0, hid_far_a)
    back_b = down(1, hid_far_b)

    def combine(chunk):
        n = SEQS[chunk]
        rows_of = e_buf[chunk][...].reshape(512, FP)
        part[FIRST[chunk] : FIRST[chunk] + n] = mm(mix[chunk][...], rows_of).astype(BF16).reshape(n, TOK, FP)

    landed(back_a)
    combine(0)
    landed(back_b)
    combine(1)

    def sum_right(k, piece):
        span = pl.ds(32 * piece, 32)
        source = part.at[11 if k == 6 else 2 * k, span]
        return remote(source, rs.at[k - 1, span], (rs_s, rs_r), 4 * (k - 1) + piece, (s, yh, zr, x, yl))

    def sum_left(k, piece):
        span = pl.ds(32 * piece, 32)
        source = part.at[11 if k == 6 else 2 * k - 1, span]
        return remote(source, rs.at[5 + k, span], (rs_s, rs_r), 4 * (5 + k) + piece, (s, yh, zl, x, yl))

    def add(slot, arrived, piece):
        span = slice(32 * piece, 32 * piece + 32)
        part[slot, span] = (part[slot, span].astype(F32) + rs[arrived, span].astype(F32)).astype(BF16)

    forward, backward = {}, {}
    for piece in range(2):
        forward[piece] = start(sum_right(6, piece))
        backward[piece + 2] = start(sum_left(6, piece + 2))
    for piece in range(2):
        forward[piece + 2] = start(sum_right(5, piece + 2))
        backward[piece] = start(sum_left(5, piece))

    def write(out, total):
        for i in range(3):
            column_block = jnp.transpose(total[:, 128 * i : 128 * (i + 1)]).astype(BF16)
            out[128 * i : min(128 * (i + 1), FB), :] = column_block if i < 2 else column_block[0 : FB - 256]

    for k in range(5, 0, -1):
        for turn_of in range(4):
            piece = turn_of
            if k < 5 or piece < 2:
                forward[piece].wait_recv()
                add(2 * k, k, piece)
                forward[piece] = start(sum_right(k, piece))
            piece = turn_of ^ 2
            if k < 5 or piece >= 2:
                backward[piece].wait_recv()
                add(2 * k - 1, 6 + k, piece)
                backward[piece] = start(sum_left(k, piece))
    wait_all(*grads)
    total = gr[0].astype(F32)
    for i in range(1, 8):
        total = total + gr[i].astype(F32)
    write(grad_out, total)
    wait_all(*forward.values(), *backward.values())
    write(moe_out, part[0].astype(F32) + rs[0].astype(F32) + rs[6].astype(F32))
    for copy in sent:
        copy.wait_send()


def on_device(
    moe_input, norm_gain, routes, route_scores, w_up, w_down, queries, keys, values, out_grad,
    w_query, w_key, w_value, w_out,
):
    tokens = jnp.transpose(moe_input[0])
    gain = norm_gain.reshape(D // 128, 128)
    routes, route_scores = jnp.transpose(routes, (2, 0, 1)), jnp.transpose(route_scores, (2, 0, 1))
    w_up, w_down = jnp.transpose(w_up, (0, 2, 1)), jnp.transpose(w_down, (0, 2, 1))
    anywhere = pl.BlockSpec(memory_space=pl.ANY)
    vmem = pl.BlockSpec(memory_space=pltpu.VMEM)
    dma = pltpu.SemaphoreType.DMA

    def vm(*shape):
        return pltpu.VMEM(shape, BF16)

    scratch = [
        vm(12, TOK, FP),
        vm(512, 896), vm(384, 640),
        vm(8, 64, FP), vm(8, 48, FP),
        vm(4, 2, 256, FP), vm(4, 2, 192, FP),
        vm(192, 128), vm(192, 128),
        vm(HB, D), vm(HB, D), vm(FB, HID), vm(FB, HID),
        vm(D, HB), vm(D, HB),
        vm(HID, FB), vm(HID, FB),
        vm(4, 256, HP), vm(4, 192, HP),
        vm(2, 256, FP), vm(2, 192, FP),
        vm(8, 64, FP), vm(8, 64, FP),
        vm(896, 512), vm(640, 512),
        vm(12, TOK, FP), vm(12, TOK, FP),
        vm(8, TOK, FP), vm(8, TOK, FP),
        vm(TOK, 256), vm(TOK, 128), vm(TOK, 128), vm(TOK, D),
        vm(D, 256), vm(D, 256), vm(256, D), vm(TOK, 512),
        dma((10,)),
        dma((24,)), dma((24,)),
        dma((16,)), dma((16,)),
        dma((1,)), dma((1,)),
        dma((6,)), dma((6,)),
        dma((8,)), dma((8,)),
        dma((8,)), dma((8,)),
        dma((16,)), dma((16,)),
        dma((48,)), dma((48,)),
        dma((8,)), dma((8,)),
    ]
    block = jax.ShapeDtypeStruct((FB, TOK), BF16)
    moe_next, grad_prev = pl.pallas_call(
        kernel,
        name="sections",
        out_shape=(block, block),
        in_specs=[vmem] * 4 + [anywhere] * 10,
        out_specs=(vmem, vmem),
        scratch_shapes=scratch,
        compiler_params=pltpu.CompilerParams(
            collective_id=0, has_side_effects=True, vmem_limit_bytes=56 * 2**20
        ),
    )(
        tokens, gain, routes, route_scores, w_up, w_down, queries[0], keys[0], values[0], out_grad[0],
        w_query, w_key, w_value, w_out,
    )
    return jnp.transpose(moe_next)[None], jnp.transpose(grad_prev)[None]


def solution(mesh):
    finer = Mesh(
        mesh.devices.reshape(2, NYH, NZ, NX, 2), ("segment", "yh", "z", "x", "yl")
    )
    expert, dp = ("yh", "z"), ("x", "yl")
    return jax.shard_map(
        on_device,
        mesh=finer,
        in_specs=(
            P("segment", expert, dp),
            P(),
            P("segment", expert, None),
            P("segment", expert, None),
            P(expert, None, dp),
            P(expert, None, dp),
            P("segment", expert, dp),
            P("segment", expert, None),
            P("segment", expert, None),
            P("segment", expert, None),
            P(None, dp),
            P(),
            P(),
            P(dp, None),
        ),
        out_specs=(P("segment", expert, dp), P("segment", expert, dp)),
        check_vma=False,
    )
```

```python
import jax
import jax.numpy as jnp
from jax import lax
from jax.experimental import pallas as pl
from jax.experimental.pallas import tpu as pltpu
from jax.sharding import Mesh
from jax.sharding import PartitionSpec as P

MESH = pl.DeviceIdType.MESH
F32 = jnp.float32
BF16 = jnp.bfloat16

D = 2688
HID = 1856
HEAD_DIM = 128
TOPK = 6
TOK = 128
CAP = 9
NZ = 12
NYH = 4
NX = 4
FB = 336
FP = 384
HB = 232
HX = 464
HP = 512
SEQS = (7, 5)
ROWS = (64, 48)
FIRST = (0, 7)
LANE_E, LANE_P, LANE_G, LANE_S = 80, 88, 96, 104


def mm(a, b):
    return lax.dot_general(a, b, (((1,), (0,)), ((), ())), preferred_element_type=F32)


def mm_nt(a, b):
    return lax.dot_general(a, b, (((1,), (1,)), ((), ())), preferred_element_type=F32)


def iota(shape, dim):
    return lax.broadcasted_iota(jnp.int32, shape, dim)


def remote(src, dst, sems, index, device):
    return pltpu.make_async_remote_copy(
        src_ref=src,
        dst_ref=dst,
        send_sem=sems[0].at[index],
        recv_sem=sems[1].at[index],
        device_id=device,
        device_id_type=MESH,
    )


def kernel(
    tok_ref, gain_ref, routes_ref, scores_ref, w_up, w_down, queries, keys, values, out_grad,
    w_query, w_key, w_value, w_out,
    moe_out, grad_out,
    ag, sel_a, sel_b, oa, ob, xa, xb, tg, rtg, wut, wuto, wdt, wdto, wu, wuo, wd, wdo, hid_a, hid_b,
    es_a, es_b, ea, eb, mix_a, mix_b, part, rs, gt, gr,
    q_v, k_v, v_v, og_v, wq_v, wkv_v, wo_v, dq_v,
    load_sem,
    ag_s, ag_r, dp_s, dp_r, tg_s, tg_r, w_s, w_r, xg_s, xg_r, hg_s, hg_r, ret_s, ret_r, rs_s, rs_r,
    gr_s, gr_r,
):
    s = lax.axis_index("segment")
    yh = lax.axis_index("yh")
    z = lax.axis_index("z")
    x = lax.axis_index("x")
    yl = lax.axis_index("yl")
    other = 1 - s
    ylo = 1 - yl
    xr, xl = lax.rem(x + 1, NX), lax.rem(x + 3, NX)
    xo = lax.rem(x + 2, NX)
    zr, zl = lax.rem(z + 1, NZ), lax.rem(z + NZ - 1, NZ)
    here = yh * 2 + yl
    sel, o_buf, x_buf, hid = (sel_a, sel_b), (oa, ob), (xa, xb), (hid_a, hid_b)
    es, e_buf, mix = (es_a, es_b), (ea, eb), (mix_a, mix_b)

    barrier = pltpu.get_barrier_semaphore()
    peers = [(s, yh, zr, x, yl), (s, yh, zl, x, yl), (s, yh, z, xr, yl), (s, yh, z, xl, yl)]
    for step in range(4):
        row = lax.rem(yh + step, NYH)
        for o in range(2):
            col = yl if o == 0 else ylo
            peers.append((other, row, z, x, col))
            if step or o:
                peers.append((s, row, z, x, col))
            if step:
                peers.append((other, yh, z, lax.rem(x + step, NX), col))
    for peer in peers:
        pl.semaphore_signal(barrier, inc=1, device_id=peer, device_id_type=MESH)

    group = pl.multiple_of((x // 2) * HEAD_DIM, HEAD_DIM)
    loads = [
        (out_grad, og_v),
        (w_out, wo_v),
        (queries, q_v),
        (keys.at[:, pl.ds(group, HEAD_DIM)], k_v),
        (values.at[:, pl.ds(group, HEAD_DIM)], v_v),
        (w_query, wq_v),
        (w_key.at[:, pl.ds(group, HEAD_DIM)], wkv_v.at[:, pl.ds(0, HEAD_DIM)]),
        (w_value.at[:, pl.ds(group, HEAD_DIM)], wkv_v.at[:, pl.ds(HEAD_DIM, HEAD_DIM)]),
        (w_up.at[yl], wut),
        (w_down.at[yl], wdt),
    ]
    loads = [pltpu.make_async_copy(a, b, load_sem.at[i]) for i, (a, b) in enumerate(loads)]
    for load in loads:
        load.start()

    lanes = iota((TOK, 128), 1)
    rows = iota((TOK, 128), 0)
    wide = tok_ref[...].astype(F32)
    squares = jnp.sum(wide * wide, axis=0, keepdims=True)
    square_hi = squares.astype(BF16).astype(F32)
    square_lo = squares - square_hi
    experts = iota((96, TOK), 0)
    hits = jnp.zeros((96, TOK), F32)
    signals = []
    for k in range(TOPK):
        hits = hits + jnp.where(routes_ref[k] == experts, 1.0, 0.0)
        signals.append(1.0 / (1.0 + jnp.exp(-scores_ref[k])))
    signal_sum = sum(signals[1:], signals[0])
    earlier = mm(hits.astype(BF16), jnp.where(rows < lanes, 1.0, 0.0).astype(BF16)) + 1.0
    info_row = iota((FP - FB, TOK), 0)
    info = jnp.where(info_row == LANE_S - LANE_E, square_hi, 0.0)
    info = jnp.where(info_row == LANE_S - LANE_E + 1, square_lo, info)
    for k in range(TOPK):
        expert = routes_ref[k]
        place = jnp.sum(jnp.where(expert == experts, earlier, 0.0), axis=0, keepdims=True)
        info = jnp.where(info_row == k, expert.astype(F32), info)
        info = jnp.where(info_row == LANE_P - LANE_E + k, place, info)
        info = jnp.where(info_row == LANE_G - LANE_E + k, signals[k] / signal_sum, info)
    gain_at = (x * 2 + yl) * FB
    gain_row, gain_lane = gain_at // 128, lax.rem(gain_at, 128)
    turn = lax.rem(128 - gain_lane, 128)
    pieces = [
        pltpu.roll(jnp.broadcast_to(gain_ref[pl.ds(jnp.minimum(gain_row + i, 20), 1), :], (8, 128)), turn, 1)
        for i in range(4)
    ]
    lane8 = iota((8, 128), 1)
    for i in range(3):
        source = wide[128 * i : 128 * (i + 1)] if i < 2 else jnp.concatenate([wide[256:], info], axis=0)
        gain = jnp.where(lane8 < 128 - gain_lane, pieces[i], pieces[i + 1])
        if i == 2:
            gain = jnp.where(lane8 < LANE_E, gain, 1.0)
        ag[0, :, 128 * i : 128 * (i + 1)] = (jnp.transpose(source) * gain[0:1]).astype(BF16)
    sel_a[...] = jnp.zeros_like(sel_a)
    sel_b[...] = jnp.zeros_like(sel_b)
    eb[:, 48:64, :] = jnp.zeros((8, 16, FP), BF16)

    pl.semaphore_wait(barrier, len(peers))

    def right(k, half):
        span = pl.ds(64 * half, 64)
        source, target = max(2 * k - 3, 0), 2 * k - 1
        return remote(ag.at[source, span], ag.at[target, span], (ag_s, ag_r), 2 * target + half, (s, yh, zr, x, yl))

    def left(k, half):
        span = pl.ds(64 * half, 64)
        source, target = 2 * k - 2, 11 if k == 6 else 2 * k
        return remote(ag.at[source, span], ag.at[target, span], (ag_s, ag_r), 2 * target + half, (s, yh, zl, x, yl))

    sent = []

    def start(copy):
        copy.start()
        sent.append(copy)
        return copy

    def wait_all(*copies):
        for copy in copies:
            copy.wait_recv()

    hops = {}
    for half in range(2):
        hops[1, half] = (start(right(1, half)), start(left(1, half)))
    up_cols = pl.ds(pl.multiple_of(s * 1408, 128), 1280)
    up_middle = pl.ds(1280, 128)
    down_rows = pl.ds(pl.multiple_of(s * 176, 16), 160)
    down_middle = pl.ds(160, 16)
    partner = (s, yh, z, x, ylo)
    swap_up = (
        start(remote(w_up.at[ylo, :, up_cols], wuto.at[:, up_cols], (w_s, w_r), 0, partner)),
        start(remote(w_up.at[ylo, :, up_middle], wuto.at[:, up_middle], (w_s, w_r), 1, partner)),
    )

    column = iota((8, 128), 0)
    my_experts = (lax.shift_right_logical(column, 1) * (2 * NZ) + 2 * z + jnp.bitwise_and(column, 1)).astype(F32)

    def take(slot):
        chunk = 0 if slot < FIRST[1] else 1
        at = slot - FIRST[chunk]
        info = jnp.transpose(ag[slot, :, 256:384].astype(F32))
        place = jnp.zeros((8, 128), F32)
        gate = jnp.zeros((8, 128), F32)
        for k in range(TOPK):
            mine = info[LANE_E + k : LANE_E + k + 1, :] == my_experts
            place = place + jnp.where(mine, info[LANE_P + k : LANE_P + k + 1, :], 0.0)
            gate = gate + jnp.where(mine, info[LANE_G + k : LANE_G + k + 1, :], 0.0)
        tg[slot * 16 : slot * 16 + 16, :] = jnp.concatenate([place, gate], axis=0).astype(BF16)
        target = jnp.where(place > 0.0, place + (at * CAP - 1.0), -1.0).astype(jnp.int32)
        count = ROWS[chunk]
        slots = iota((count, 128), 0)
        for y in range(8):
            block = jnp.where(slots == target[y : y + 1, :], 1.0, 0.0).astype(BF16)
            sel[chunk][y * count : (y + 1) * count, at * TOK : (at + 1) * TOK] = block

    def dispatch(chunk):
        n, count = SEQS[chunk], ROWS[chunk]
        blocks = ag[FIRST[chunk] : FIRST[chunk] + n].reshape(n * TOK, FP)
        picked = mm(sel[chunk][...], blocks).astype(BF16)
        o_buf[chunk][...] = picked.reshape(8, count, FP)
        copies = []
        for step in range(4):
            row = lax.rem(yh + step, NYH)
            for o in range(2):
                col = yl if o == 0 else ylo
                copies.append(
                    start(
                        remote(
                            o_buf[chunk].at[row * 2 + col],
                            x_buf[chunk].at[x, yl, pl.ds(pl.multiple_of(yh * count, 16), count)],
                            (dp_s, dp_r),
                            chunk * 8 + step * 2 + o,
                            (other, row, z, x, col),
                        )
                    )
                )
        return copies

    d_kv = [jnp.zeros((TOK, HEAD_DIM), F32), jnp.zeros((TOK, HEAD_DIM), F32)]
    d_attn = {}

    def attention_grad(h):
        if h == 0:
            for load in loads[:2]:
                load.wait()
        d_attn[h] = mm_nt(og_v[...], wo_v[h * HEAD_DIM : (h + 1) * HEAD_DIM, :]).astype(BF16)

    def attention_in(h):
        if h == 0:
            for load in loads[2:5]:
                load.wait()
        key, value = k_v[...], v_v[...]
        scale = HEAD_DIM ** (-0.5)
        span = slice(h * HEAD_DIM, (h + 1) * HEAD_DIM)
        query, grad = q_v[:, span], d_attn[h]
        score = jnp.where(lanes <= rows, mm_nt(query, key) * scale, -jnp.inf)
        raised = jnp.exp(score - jnp.max(score, axis=1, keepdims=True))
        weights = raised / jnp.sum(raised, axis=1, keepdims=True)
        d_weights = mm_nt(grad, value)
        delta = jnp.sum(weights * d_weights, axis=1, keepdims=True)
        d_scores = weights * (d_weights - delta)
        dq_v[:, span] = (mm(d_scores.astype(BF16), key) * scale).astype(BF16)
        d_kv[0] = d_kv[0] + mm(jnp.transpose(d_scores).astype(BF16), query)
        d_kv[1] = d_kv[1] + mm(jnp.transpose(weights).astype(BF16), grad)
        if h == 1:
            dq_v[:, 256:384] = (d_kv[0] * scale).astype(BF16)
            dq_v[:, 384:512] = d_kv[1].astype(BF16)

    grads = []

    def attention_out(step):
        if step == 2:
            for load in loads[5:8]:
                load.wait()
        to = lax.rem(x + step, NX)
        for o in range(2):
            col = yl if o == 0 else ylo
            block = pl.ds(pl.multiple_of((to * 2 + col) * FB, 16), FB)
            term = mm_nt(dq_v[:, 0:256], wq_v[block, :]) + mm_nt(dq_v[:, 256:512], wkv_v[block, :])
            gt[step * 2 + o, :, 0:FB] = term.astype(BF16)
            grads.append(
                start(remote(gt.at[step * 2 + o], gr.at[step * 2 + o], (gr_s, gr_r), step * 2 + o, (other, yh, z, to, col)))
            )

    def hop(k, half):
        wait_all(*hops[k, half])
        if k < 5:
            hops[k + 1, half] = (start(right(k + 1, half)), start(left(k + 1, half)))
        elif k == 5:
            hops[6, half] = (start(left(6, 1) if half else right(6, 0)),)

    def spread(buf, sems, chunk):
        a = start(remote(buf.at[x], buf.at[x], sems, chunk * 4, (s, yh, z, xr, yl)))
        b = start(remote(buf.at[x], buf.at[x], sems, chunk * 4 + 1, (s, yh, z, xl, yl)))
        return a, b

    def relay(buf, sems, chunk, nearer, lower, upper):
        nearer[0].wait_recv()
        a = start(remote(buf.at[(xl, *lower)], buf.at[(xl, *lower)], sems, chunk * 4 + 2, (s, yh, z, xr, yl)))
        nearer[1].wait_recv()
        b = start(remote(buf.at[(xr, *upper)], buf.at[(xr, *upper)], sems, chunk * 4 + 3, (s, yh, z, xl, yl)))
        return a, b

    up_sems, hid_sems = (xg_s, xg_r), (hg_s, hg_r)
    take(0)
    attention_grad(0)
    hop(1, 0)
    hop(1, 1)
    take(1)
    take(2)
    hop(2, 0)
    attention_grad(1)
    hop(2, 1)
    take(3)
    take(4)
    hop(3, 0)
    attention_in(0)
    hop(3, 1)
    take(5)
    take(6)
    arrive_a = dispatch(0)
    hop(4, 0)
    attention_in(1)
    hop(4, 1)
    take(7)
    take(8)
    hop(5, 0)
    attention_out(2)
    hop(5, 1)
    take(9)
    take(10)
    attention_out(1)
    hop(6, 0)
    hop(6, 1)
    take(11)
    arrive_b = dispatch(1)
    table = start(remote(tg, rtg, (tg_s, tg_r), 0, (other, yh, z, x, yl)))
    wait_all(*arrive_a)
    near_a = spread(xa, up_sems, 0)
    wait_all(*swap_up)
    share_up = start(remote(wuto.at[:, up_cols], wuto.at[:, up_cols], (w_s, w_r), 2, (other, yh, z, x, yl)))
    attention_out(3)
    attention_out(0)
    unit = jnp.where(lanes == rows, 1.0, 0.0).astype(BF16)

    def turn_up(source, target):
        def step(i, carry):
            span = pl.ds(pl.multiple_of(i * 128, 128), 128)
            target[span, :] = mm_nt(unit, source[:, span]).astype(BF16)
            return carry

        lax.fori_loop(0, D // 128, step, 0)

    def turn_down(source, target):
        def step(i, carry):
            span = pl.ds(pl.multiple_of(i * 128, 128), 128)
            target[span, :] = mm_nt(unit, source[:, span]).astype(BF16)
            return carry

        lax.fori_loop(0, HID // 128, step, 0)
        target[1792:1856, :] = mm_nt(unit[0:64, 0:64], source[:, 1792:1856]).astype(BF16)

    loads[8].wait()
    turn_up(wut, wu)
    wait_all(*arrive_b)
    near_b = spread(xb, up_sems, 1)
    swap_down = (
        start(remote(w_down.at[ylo, down_rows], wdto.at[down_rows], (w_s, w_r), 3, partner)),
        start(remote(w_down.at[ylo, down_middle], wdto.at[down_middle], (w_s, w_r), 4, partner)),
    )
    far_a = relay(xa, up_sems, 0, near_a, (0,), (1,))

    table.wait_recv()

    def mixing(slot, turned, base):
        chunk = 0 if slot < FIRST[1] else 1
        at = slot - FIRST[chunk]
        for pair in range(4):
            c = slot * 16 - base + 2 * pair
            low = lanes < 64
            place = jnp.where(low, turned[:, c : c + 1], turned[:, c + 1 : c + 2])
            gate = jnp.where(low, turned[:, c + 8 : c + 9], turned[:, c + 9 : c + 10])
            slots = jnp.bitwise_and(lanes, 63).astype(F32)
            hit = jnp.logical_and(place > 0.0, slots == place + (at * CAP - 1.0))
            mix[chunk][at * TOK : (at + 1) * TOK, pair * 128 : (pair + 1) * 128] = jnp.where(hit, gate, 0.0).astype(BF16)

    turned = jnp.transpose(rtg[0:128, :].astype(F32))
    for slot in range(8):
        mixing(slot, turned, 0)
    turned = jnp.transpose(rtg[64:192, :].astype(F32))
    for slot in range(8, 12):
        mixing(slot, turned, 64)

    share_up.wait_recv()
    turn_up(wuto, wuo)
    far_b = relay(xb, up_sems, 1, near_b, (0,), (1,))

    def place_hidden(which):
        return jnp.where(iota((HB, HP), 1) == iota((HB, HP), 0) + which * HB, 1.0, 0.0).astype(BF16)

    def up(chunk, far):
        buf = x_buf[chunk]
        count = 4 * ROWS[chunk]
        mine = jnp.zeros((count, HB), F32)
        theirs = jnp.zeros((count, HB), F32)
        sums = jnp.zeros((count, 128), F32)
        for index, owner in enumerate((x, xl, xr, xo)):
            for part_of in range(2):
                if index == 3:
                    far[part_of].wait_recv()
                first = pl.ds(pl.multiple_of((owner * 2 + part_of) * FB, 16), FB)
                block = buf[owner, part_of, :, 0:FB]
                mine = mine + mm(block, wu[first, :])
                theirs = theirs + mm(block, wuo[first, :])
                sums = sums + buf[owner, part_of, :, 256:384].astype(F32)
        lane = iota((count, 128), 1)
        kept = jnp.where(jnp.logical_or(lane == LANE_S, lane == LANE_S + 1), sums, 0.0)
        inverse = 1.0 / jnp.sqrt(jnp.sum(kept, axis=1, keepdims=True) / D + 1e-5)
        mine = jnp.square(jnp.maximum(mine * inverse, 0.0)).astype(BF16)
        theirs = jnp.square(jnp.maximum(theirs * inverse, 0.0)).astype(BF16)
        hid[chunk][x] = (mm(mine, place_hidden(yl)) + mm(theirs, place_hidden(ylo))).astype(BF16)
        return spread(hid[chunk], hid_sems, chunk)

    hid_near_a = up(0, far_a)
    hid_near_b = up(1, far_b)
    wait_all(*swap_down)
    share_down = start(remote(wdto.at[down_rows], wdto.at[down_rows], (w_s, w_r), 5, (other, yh, z, x, yl)))
    hid_far_a = relay(hid_a, hid_sems, 0, hid_near_a, (pl.ds(0, 128),), (pl.ds(128, 128),))
    loads[9].wait()
    turn_down(wdt, wd)
    hid_far_b = relay(hid_b, hid_sems, 1, hid_near_b, (pl.ds(0, 96),), (pl.ds(96, 96),))
    share_down.wait_recv()
    turn_down(wdto, wdo)

    def down(chunk, far):
        count = ROWS[chunk]
        buf = hid[chunk]
        mine = jnp.zeros((4 * count, FB), F32)
        theirs = jnp.zeros((4 * count, FB), F32)
        for index, owner in enumerate((x, xl, xr, xo)):
            if index == 3:
                far[0].wait_recv()
                far[1].wait_recv()
            first = pl.ds(pl.multiple_of(owner * HX, 16), HX)
            block = buf[owner, :, 0:HX]
            mine = mine + mm(block, wd[first, :])
            theirs = theirs + mm(block, wdo[first, :])
        es[chunk][0, :, 0:FB] = mine.astype(BF16)
        es[chunk][1, :, 0:FB] = theirs.astype(BF16)
        copies = []
        for step in range(4):
            row = lax.rem(yh + step, NYH)
            span = pl.ds(pl.multiple_of(row * count, 16), count)
            for o in range(2):
                source = es[chunk].at[o, span]
                target = e_buf[chunk].at[here, pl.ds(0, count)]
                index = chunk * 8 + step * 2 + o
                if step or o:
                    copies.append(
                        start(remote(source, target, (ret_s, ret_r), index, (s, row, z, x, yl if o == 0 else ylo)))
                    )
                else:
                    local = pltpu.make_async_copy(source, target, ret_r.at[index])
                    local.start()
                    copies.append(local)
        return copies

    def landed(copies):
        copies[0].wait()
        for copy in copies[1:]:
            copy.wait_recv()

    back_a = down(0, hid_far_a)
    back_b = down(1, hid_far_b)

    def combine(chunk):
        n = SEQS[chunk]
        rows_of = e_buf[chunk][...].reshape(512, FP)
        part[FIRST[chunk] : FIRST[chunk] + n] = mm(mix[chunk][...], rows_of).astype(BF16).reshape(n, TOK, FP)

    landed(back_a)
    combine(0)
    landed(back_b)
    combine(1)

    def sum_right(k, piece):
        span = pl.ds(32 * piece, 32)
        source = part.at[11 if k == 6 else 2 * k, span]
        return remote(source, rs.at[k - 1, span], (rs_s, rs_r), 4 * (k - 1) + piece, (s, yh, zr, x, yl))

    def sum_left(k, piece):
        span = pl.ds(32 * piece, 32)
        source = part.at[11 if k == 6 else 2 * k - 1, span]
        return remote(source, rs.at[5 + k, span], (rs_s, rs_r), 4 * (5 + k) + piece, (s, yh, zl, x, yl))

    def add(slot, arrived, piece):
        span = slice(32 * piece, 32 * piece + 32)
        part[slot, span] = (part[slot, span].astype(F32) + rs[arrived, span].astype(F32)).astype(BF16)

    forward, backward = {}, {}
    for piece in range(2):
        forward[piece] = start(sum_right(6, piece))
        backward[piece + 2] = start(sum_left(6, piece + 2))
    for piece in range(2):
        forward[piece + 2] = start(sum_right(5, piece + 2))
        backward[piece] = start(sum_left(5, piece))

    def write(out, total):
        for i in range(3):
            column_block = jnp.transpose(total[:, 128 * i : 128 * (i + 1)]).astype(BF16)
            out[128 * i : min(128 * (i + 1), FB), :] = column_block if i < 2 else column_block[0 : FB - 256]

    for k in range(5, 0, -1):
        for turn_of in range(4):
            piece = turn_of
            if k < 5 or piece < 2:
                forward[piece].wait_recv()
                add(2 * k, k, piece)
                forward[piece] = start(sum_right(k, piece))
            piece = turn_of ^ 2
            if k < 5 or piece >= 2:
                backward[piece].wait_recv()
                add(2 * k - 1, 6 + k, piece)
                backward[piece] = start(sum_left(k, piece))
    wait_all(*grads)
    total = gr[0].astype(F32)
    for i in range(1, 8):
        total = total + gr[i].astype(F32)
    write(grad_out, total)
    wait_all(*forward.values(), *backward.values())
    write(moe_out, part[0].astype(F32) + rs[0].astype(F32) + rs[6].astype(F32))
    for copy in sent:
        copy.wait_send()


def on_device(
    moe_input, norm_gain, routes, route_scores, w_up, w_down, queries, keys, values, out_grad,
    w_query, w_key, w_value, w_out,
):
    tokens = jnp.transpose(moe_input[0])
    gain = norm_gain.reshape(D // 128, 128)
    routes, route_scores = jnp.transpose(routes, (2, 0, 1)), jnp.transpose(route_scores, (2, 0, 1))
    w_up, w_down = jnp.transpose(w_up, (0, 2, 1)), jnp.transpose(w_down, (0, 2, 1))
    anywhere = pl.BlockSpec(memory_space=pl.ANY)
    vmem = pl.BlockSpec(memory_space=pltpu.VMEM)
    dma = pltpu.SemaphoreType.DMA

    def vm(*shape):
        return pltpu.VMEM(shape, BF16)

    scratch = [
        vm(12, TOK, FP),
        vm(512, 896), vm(384, 640),
        vm(8, 64, FP), vm(8, 48, FP),
        vm(4, 2, 256, FP), vm(4, 2, 192, FP),
        vm(192, 128), vm(192, 128),
        vm(HB, D), vm(HB, D), vm(FB, HID), vm(FB, HID),
        vm(D, HB), vm(D, HB),
        vm(HID, FB), vm(HID, FB),
        vm(4, 256, HP), vm(4, 192, HP),
        vm(2, 256, FP), vm(2, 192, FP),
        vm(8, 64, FP), vm(8, 64, FP),
        vm(896, 512), vm(640, 512),
        vm(12, TOK, FP), vm(12, TOK, FP),
        vm(8, TOK, FP), vm(8, TOK, FP),
        vm(TOK, 256), vm(TOK, 128), vm(TOK, 128), vm(TOK, D),
        vm(D, 256), vm(D, 256), vm(256, D), vm(TOK, 512),
        dma((10,)),
        dma((24,)), dma((24,)),
        dma((16,)), dma((16,)),
        dma((1,)), dma((1,)),
        dma((6,)), dma((6,)),
        dma((8,)), dma((8,)),
        dma((8,)), dma((8,)),
        dma((16,)), dma((16,)),
        dma((48,)), dma((48,)),
        dma((8,)), dma((8,)),
    ]
    block = jax.ShapeDtypeStruct((FB, TOK), BF16)
    moe_next, grad_prev = pl.pallas_call(
        kernel,
        name="sections",
        out_shape=(block, block),
        in_specs=[vmem] * 4 + [anywhere] * 10,
        out_specs=(vmem, vmem),
        scratch_shapes=scratch,
        compiler_params=pltpu.CompilerParams(
            collective_id=0, has_side_effects=True, vmem_limit_bytes=56 * 2**20
        ),
    )(
        tokens, gain, routes, route_scores, w_up, w_down, queries[0], keys[0], values[0], out_grad[0],
        w_query, w_key, w_value, w_out,
    )
    return jnp.transpose(moe_next)[None], jnp.transpose(grad_prev)[None]


def solution(mesh):
    finer = Mesh(
        mesh.devices.reshape(2, NYH, NZ, NX, 2), ("segment", "yh", "z", "x", "yl")
    )
    expert, dp = ("yh", "z"), ("x", "yl")
    return jax.shard_map(
        on_device,
        mesh=finer,
        in_specs=(
            P("segment", expert, dp),
            P(),
            P("segment", expert, None),
            P("segment", expert, None),
            P(expert, None, dp),
            P(expert, None, dp),
            P("segment", expert, dp),
            P("segment", expert, None),
            P("segment", expert, None),
            P("segment", expert, None),
            P(None, dp),
            P(),
            P(),
            P(dp, None),
        ),
        out_specs=(P("segment", expert, dp), P("segment", expert, dp)),
        check_vma=False,
    )
```
